32 devices in a mesh: lat: 4 (over y, x), lev: 8 (over z, core).
Axes of the slice: x: 2, y: 2, z: 4, core: 2. Of those that a mesh axis runs over, the one named last changes fastest.
Arguments:
- adjoint_grid: bfloat16 [128, 768, 1536], P('lev', 'lat'), may hold values from -6 to 6
- wind: bfloat16 [128, 768, 1536], P('lev', 'lat'), may hold values from -6 to 6
- legendre: bfloat16 [1024, 768, 520], P(('lat', 'lev')), may hold values from -0.21875 to 0.21875
- vertical: bfloat16 [16, 128, 128], replicated, may hold values from -0.5 to 0.5
- pair_table: int32 [256], replicated, may hold values from 0 to 255, each once
- degree_matrix: int32 [512], replicated, may hold values from 0 to 15
Outputs:
- adjoint_out: bfloat16 [128, 768, 1536], P('lev', 'lat')
The draws below stay inside these ranges and needn't reach their ends.
Inputs may be any that keep to these rules, and one draw needn't show every extreme that they name: `pair_table`: the values are distinct: every pair (m, 511 - m) with m < 256 stands in exactly one slot.
All inputs are finite; a program needn't handle non-finite values.
Results may differ from the reference program's by a relative error of at most 0.008.
Values may be sent and summed in bfloat16 or wider, within the bound.
No kernel may reach another device: no remote copies, remote signals or barrier semaphores. Data moves between devices by JAX's collectives and lax.ppermute only.
A program may use at most 128 MiB of HBM per device.

```python
import math
import jax
import jax.numpy as jnp
from jax import lax

LAT = 768
LON = 1536
LEV = 128
N = 512
NMAT = 16
PAIRS = 256
KP = 520


def plant(entries, key, low, high):
    dims = entries.shape
    index_at = [jax.random.randint(jax.random.fold_in(key, axis), (), 0, dims[axis]) for axis in range(len(dims))]
    entries = entries.at[tuple(index_at)].set(low)
    longest = dims.index(max(dims))
    index_at[longest] = (index_at[longest] + 1) % dims[longest]
    return entries.at[tuple(index_at)].set(high)


def block_scale(key, extent, shards, least, top_value):
    def one(dim, parts):
        heights = jax.random.uniform(jax.random.fold_in(jax.random.fold_in(key, 6), dim), (parts,), jnp.float32, least / len(shards), top_value / len(shards))
        return jnp.repeat(jnp.exp(heights), extent[dim] // parts).reshape((-1,) + (1,) * (len(extent) - dim - 1))

    gain = one(*shards[0])
    for cut in shards[1:]:
        gain = gain * one(*cut)
    return gain


def centred(stream_key, shape, scale, limit, cuts=(), kind=jnp.bfloat16):
    drawn = jax.random.normal(stream_key, shape, jnp.float32) * scale
    if len(cuts) > 0:
        drawn = block_scale(stream_key, shape, cuts, -0.22, 0.18) * drawn
    return jnp.clip(drawn, min=-limit, max=limit).astype(kind)


def setup_inputs(seed: int = 0) -> dict:
    splits = jax.random.split(jax.random.key(seed), 7)
    return {
        "adjoint_grid": centred(splits[0], (LEV, LAT, LON), 1.0, 6.0, ((0, 8), (1, 4))),
        "wind": centred(splits[1], (LEV, LAT, LON), 1.0, 6.0, ((0, 8), (1, 4))),
        "legendre": centred(splits[2], (4 * PAIRS, LAT, KP), LAT ** -0.5, 0.21875, ((0, 32),)),
        "vertical": centred(splits[3], (NMAT, LEV, LEV), LEV ** -0.5, 0.5),
        "pair_table": jax.random.permutation(splits[4], PAIRS).astype(jnp.int32),
        "degree_matrix": plant(jax.random.randint(splits[5], (N,), 0, NMAT), jax.random.fold_in(splits[5], 1), 0, NMAT - 1).astype(jnp.int32),
    }


def fourier_basis(wavenumbers, points):
    longitude = jnp.arange(points, dtype=jnp.int32)
    phases = wavenumbers[:, :, None] * longitude[None, None, :] % points
    angles = phases.astype(jnp.float32) * (2.0 * jnp.pi / points)
    basis = jnp.stack([jnp.cos(angles), -jnp.sin(angles)], axis=2)
    return basis.reshape(-1, points)

def member_layout(lower_wave, row_start, row_total):
    packed_buffer = row_start + jnp.arange(row_total, dtype=jnp.int32)
    first_member = packed_buffer[None, :] < (N - lower_wave)[:, None]
    second_member = jnp.logical_not(first_member) & (packed_buffer[None, :] <= N)
    degree = jnp.where(first_member, lower_wave[:, None] + packed_buffer[None, :], packed_buffer[None, :] - 1)
    degree = jnp.clip(degree, 0, N - 1).astype(jnp.int32)
    return (first_member, second_member, degree)

def reference(adjoint_grid, wind, legendre, vertical, pair_table, degree_matrix):
    wavenumbers = jnp.stack([pair_table, N - 1 - pair_table], axis=1).astype(jnp.int32)
    basis = fourier_basis(wavenumbers, LON)
    analysis_table = (basis * (1.0 / math.sqrt(LON))).astype(jnp.bfloat16)
    synthesis_table = (basis * (1.0 / math.sqrt(N))).astype(jnp.bfloat16)
    flattened = adjoint_grid.reshape(LEV * LAT, LON)
    fourier = jnp.dot(flattened, analysis_table.T, preferred_element_type=jnp.float32).astype(jnp.bfloat16)
    fourier = fourier.reshape(LEV, LAT, 4 * PAIRS).transpose(2, 0, 1)
    column = jnp.arange(4 * PAIRS, dtype=jnp.int32)
    lower_cols = pair_table[column // 4]
    member = column // 2 % 2
    first_member, second_member, degree = member_layout(lower_cols, 0, KP)
    own_rows = jnp.where((member == 0)[:, None], first_member, second_member).astype(jnp.float32)
    matrix_index = degree_matrix[degree]
    vertical_full = vertical.astype(jnp.float32)

    def one_column(operands):
        table_col, local_column, index_col, field_col = operands
        table_full = table_col.astype(jnp.float32)
        spectral_state = jnp.einsum('lk,vl->kv', table_full, field_col.astype(jnp.float32)) * local_column[:, None]
        spectral_half = lax.optimization_barrier(spectral_state.astype(jnp.bfloat16)).astype(jnp.float32)
        matrices = vertical_full[index_col]
        solved_columns = jnp.einsum('kv,kvo->ko', spectral_half, matrices)
        solved_half = lax.optimization_barrier(solved_columns.astype(jnp.bfloat16)).astype(jnp.float32)
        return jnp.einsum('lk,ko->ol', table_full, solved_half).astype(jnp.bfloat16)
    coeffs = lax.map(one_column, (legendre, own_rows, matrix_index, fourier))
    columns = coeffs.transpose(1, 2, 0).reshape(LEV * LAT, 4 * PAIRS)
    regridded = jnp.dot(columns, synthesis_table, preferred_element_type=jnp.float32).reshape(LEV, LAT, LON)
    return (regridded * wind.astype(jnp.float32)).astype(jnp.bfloat16)
```

```python
import functools
import math

import jax
import jax.numpy as jnp
from jax import lax
from jax.experimental import pallas as pl
from jax.experimental.pallas import tpu as pltpu
from jax.sharding import PartitionSpec as P

N = 512
CORES = 2
ROWS = 8
LANES = 128
VMEM = 48 * 2**20


def fourier_basis(wavenumbers, points):
    longitude = jnp.arange(points, dtype=jnp.int32)
    phases = wavenumbers[:, :, None] * longitude[None, None, :] % points
    angles = phases.astype(jnp.float32) * (2.0 * jnp.pi / points)
    basis = jnp.stack([jnp.cos(angles), -jnp.sin(angles)], axis=2)
    return basis.reshape(-1, points)


def member_layout(lower_wave, row_total):
    packed_buffer = jnp.arange(row_total, dtype=jnp.int32)
    first_member = packed_buffer[None, :] < (N - lower_wave)[:, None]
    second_member = jnp.logical_not(first_member) & (packed_buffer[None, :] <= N)
    degree = jnp.where(
        first_member, lower_wave[:, None] + packed_buffer[None, :], packed_buffer[None, :] - 1
    )
    degree = jnp.clip(degree, 0, N - 1)
    return (first_member, second_member, degree)


def solve_columns(spectral_state, matrix_index, vertical):

    def add_matrix(operator_index, running):
        product = jnp.einsum(
            "xjm,mg->xjg",
            spectral_state,
            vertical[operator_index],
            preferred_element_type=jnp.float32,
        )
        return running + jnp.where((matrix_index == operator_index)[:, :, None], product, 0.0)

    zero_sums = jnp.zeros(spectral_state.shape, jnp.float32)
    return lax.fori_loop(0, vertical.shape[0], add_matrix, zero_sums).astype(jnp.bfloat16)


def general_body(adjoint_grid, wind, legendre, vertical, pair_table, degree_matrix):
    vertical_level_rows, lat_rows, points = adjoint_grid.shape
    lat_devices = lax.axis_size("lat")
    lev_devices = lax.axis_size("lev")
    slots = legendre.shape[0]
    all_lats = legendre.shape[1]
    packed_rows = legendre.shape[2]
    levels = vertical.shape[1]
    wavenumbers = jnp.stack([pair_table, N - 1 - pair_table], axis=1)
    basis = fourier_basis(wavenumbers, points)
    analysis_table = (basis * (1.0 / math.sqrt(points))).astype(jnp.bfloat16)
    synthesis_table = (basis * (1.0 / math.sqrt(N))).astype(jnp.bfloat16)
    fourier = jnp.einsum(
        "cx,vlx->cvl", analysis_table, adjoint_grid, preferred_element_type=jnp.float32
    )
    fourier = fourier.astype(jnp.bfloat16).reshape(
        lat_devices, lev_devices, slots, vertical_level_rows, lat_rows
    )
    moved = lax.all_to_all(
        lax.all_to_all(fourier, "lev", split_axis=1, concat_axis=3, tiled=True),
        "lat",
        split_axis=0,
        concat_axis=4,
        tiled=True,
    )
    field_stack = moved.reshape(slots, levels, all_lats)
    first_slot = (lax.axis_index("lat") * lev_devices + lax.axis_index("lev")) * slots
    column = first_slot + jnp.arange(slots, dtype=jnp.int32)
    lower_cols = jnp.take(pair_table, column // 4)
    member = column // 2 % 2
    first_member, second_member, degree = member_layout(lower_cols, packed_rows)
    own_rows = jnp.where((member == 0)[:, None], first_member, second_member).astype(jnp.float32)
    spectral_state = jnp.einsum(
        "peq,pae->pqa", legendre, field_stack, preferred_element_type=jnp.float32
    )
    spectral_state = (spectral_state * own_rows[:, :, None]).astype(jnp.bfloat16)
    matrix_index = jnp.take(degree_matrix, degree)
    solved_columns = solve_columns(spectral_state, matrix_index, vertical)
    gridpoint_coefficients = jnp.einsum(
        "ncb,nba->nac", legendre, solved_columns, preferred_element_type=jnp.float32
    )
    gridpoint_coefficients = gridpoint_coefficients.astype(jnp.bfloat16).reshape(
        1, 1, slots, levels, all_lats
    )
    returned = lax.all_to_all(
        lax.all_to_all(gridpoint_coefficients, "lat", split_axis=4, concat_axis=0, tiled=True),
        "lev",
        split_axis=3,
        concat_axis=1,
        tiled=True,
    )
    columns = returned.reshape(lat_devices * lev_devices * slots, vertical_level_rows, lat_rows)
    regridded = jnp.einsum(
        "cvl,cx->vlx", columns, synthesis_table, preferred_element_type=jnp.float32
    )
    return (regridded * wind.astype(jnp.float32)).astype(jnp.bfloat16)


def dot(a, b, dims):
    return lax.dot_general(a, b, (dims, ((), ())), preferred_element_type=jnp.float32)


def make_table(wave, points, scale):
    rows = wave.shape[0]
    unit = 2.0 * math.pi / points
    lane = lax.broadcasted_iota(jnp.int32, (rows, LANES), 1).astype(jnp.float32)
    waves = jnp.broadcast_to(wave, (rows, LANES)).astype(jnp.float32)

    def turn(steps):
        return (steps - points * jnp.floor(steps * (1.0 / points))) * unit

    fine = turn(waves * lane)
    coarse = turn(waves * (lane * LANES))
    cos_fine, sin_fine = jnp.cos(fine), jnp.sin(fine)
    cos_coarse, sin_coarse = jnp.cos(coarse) * scale, jnp.sin(coarse) * scale
    part = lax.broadcasted_iota(jnp.int32, (rows, LANES), 0) % 2
    by_cos = jnp.where(part == 0, cos_coarse, -sin_coarse)
    by_sin = jnp.where(part == 0, -sin_coarse, -cos_coarse)
    pieces = [
        by_cos[:, a : a + 1] * cos_fine + by_sin[:, a : a + 1] * sin_fine
        for a in range(points // LANES)
    ]
    return jnp.concatenate(pieces, axis=1).astype(jnp.bfloat16)


def fourier_kernel(parity_ref, wave_ref, grid_ref, out_ref, table_ref):
    step = pl.program_id(0)
    points = grid_ref.shape[-1]

    @pl.when(step == 0)
    def _():
        table_ref[...] = make_table(wave_ref[...], points, 1.0 / math.sqrt(points))

    half = LANES // 2
    whole = pl.ds(pl.multiple_of(half * parity_ref[0], half), LANES)
    rest = pl.ds(pl.multiple_of(LANES * (1 - parity_ref[0]), half), half)
    rows = []
    for j in range(2):
        rows += [grid_ref[t, 0, j, whole, :] for t in range(2)]
        rows += [grid_ref[t, 0, j, rest, :] for t in range(2)]
    sums = dot(table_ref[...], jnp.concatenate(rows, axis=0), ((1,), (1,)))
    sums = sums.reshape(-1, ROWS, sums.shape[1])
    tiles = [sums[:, :, t * LANES : (t + 1) * LANES] for t in range(6)]
    at = pl.ds(pl.multiple_of(step * 6 * ROWS, 6 * ROWS), 6 * ROWS)
    out_ref[:, at, :] = jnp.concatenate(tiles, axis=1).astype(jnp.bfloat16)


def fourier_chunk(grid, wave, parity):
    _, steps, _, lat_rows, points = grid.shape
    columns = wave.shape[0]
    rows = steps * 6 * ROWS
    slots = columns // ROWS
    return pl.pallas_call(
        fourier_kernel,
        out_shape=jax.ShapeDtypeStruct((slots, rows, LANES), jnp.bfloat16),
        grid_spec=pltpu.PrefetchScalarGridSpec(
            num_scalar_prefetch=1,
            grid=(steps,),
            in_specs=[
                pl.BlockSpec((columns, 1), lambda s, _: (0, 0)),
                pl.BlockSpec((2, 1, 2, lat_rows, points), lambda s, _: (0, s, 0, 0, 0)),
            ],
            out_specs=pl.BlockSpec((slots, rows, LANES), lambda s, _: (0, 0, 0)),
            scratch_shapes=[pltpu.VMEM((columns, points), jnp.bfloat16)],
        ),
        compiler_params=pltpu.CompilerParams(vmem_limit_bytes=VMEM),
        cost_estimate=pl.CostEstimate(
            flops=2 * columns * grid.size, bytes_accessed=2 * grid.size, transcendentals=0
        ),
        name="fourier_chunk",
    )(parity, wave, grid)


def table_kernel(wave_ref, out_ref):
    out_ref[...] = make_table(wave_ref[...], out_ref.shape[1], 1.0 / math.sqrt(N))


def synthesis_rows(wave, points, block):
    columns = wave.shape[0]
    return pl.pallas_call(
        table_kernel,
        out_shape=jax.ShapeDtypeStruct((columns, points), jnp.bfloat16),
        grid=(columns // block,),
        in_specs=[pl.BlockSpec((block, 1), lambda s: (s, 0))],
        out_specs=pl.BlockSpec((block, points), lambda s: (s, 0)),
        compiler_params=pltpu.CompilerParams(vmem_limit_bytes=VMEM),
        name="synthesis_rows",
    )(wave)


def spectral_kernel(
    lower_ref, field_ref, table_ref, vertical_ref, first_ref, second_ref, out_ref, field_all, out_all
):
    pair = pl.program_id(0)
    lats, levs, wire_rows, _ = field_ref.shape
    stride = 3 * ROWS
    count = levs * wire_rows // stride
    block = levs * wire_rows
    half = LANES // 2
    packed = table_ref.shape[1]
    matrices = vertical_ref.shape[0] // LANES

    @pl.when(pair == 0)
    def _():
        field_all[...] = field_ref[...].reshape(field_all.shape).astype(jnp.float32)

    left = lax.broadcasted_iota(jnp.int32, (count, LANES), 1) < half
    lower = lower_ref[pair]
    row = lax.broadcasted_iota(jnp.int32, (packed, LANES), 0)
    own = row < N - lower
    valid = row <= N
    operator = jnp.where(own, first_ref[pl.ds(lower, packed), :], second_ref[...])

    def at(lat, t, column):
        return pl.ds(lat * block + t * ROWS + column, count, stride=stride)

    def swap(x):
        return pltpu.roll(x, half, 1)

    def read_field(column):
        tiles = []
        for lat in range(0, lats, 2):
            low = field_all[at(lat, 2, column), :]
            high = field_all[at(lat + 1, 2, column), :]
            middle = [jnp.where(left, low, swap(high)), jnp.where(left, swap(low), high)]
            tiles.append([field_all[at(lat, t, column), :] for t in range(2)])
            tiles.append(middle)
            tiles.append([field_all[at(lat + 1, t, column), :] for t in range(2)])
        levels = [jnp.concatenate([tile[t] for tile in tiles], axis=1) for t in range(2)]
        return jnp.concatenate(levels, axis=0).astype(jnp.bfloat16)

    def write_field(column, value):
        for lat in range(0, lats, 2):
            first = lat // 2 * 3 * LANES
            tile = [value[:, first + i * LANES : first + (i + 1) * LANES] for i in range(3)]
            parts = [[x[:count], x[count:]] for x in tile]
            for t in range(2):
                out_all[at(lat, t, column), :] = parts[0][t]
                out_all[at(lat + 1, t, column), :] = parts[2][t]
            out_all[at(lat, 2, column), :] = jnp.where(left, parts[1][0], swap(parts[1][1]))
            out_all[at(lat + 1, 2, column), :] = jnp.where(left, swap(parts[1][0]), parts[1][1])

    for r in range(2):
        state = []
        for e in range(2):
            field = read_field(4 * pair + 2 * e + r)
            state.append(dot(table_ref[2 * e + r], field, ((1,), (1,))))
        spectral = jnp.where(own, state[0], jnp.where(valid, state[1], 0.0))
        spectral = spectral.astype(jnp.bfloat16).astype(jnp.float32)
        spread = [
            jnp.where(operator == g, spectral, 0.0).astype(jnp.bfloat16) for g in range(matrices)
        ]
        solved = dot(jnp.concatenate(spread, axis=1), vertical_ref[...], ((1,), (0,)))
        for e in range(2):
            mine = jnp.where(own, solved, 0.0) if e == 0 else jnp.where(own, 0.0, solved)
            value = dot(mine.astype(jnp.bfloat16), table_ref[2 * e + r], ((0,), (0,)))
            write_field(4 * pair + 2 * e + r, value)

    @pl.when(pair == pl.num_programs(0) - 1)
    def _():
        out_ref[...] = out_all[...].astype(jnp.bfloat16).reshape(out_ref.shape)


def spectral_chunk(field, table, vertical, first, second, lower, chunk):
    lats, levs, wire_rows, _ = field.shape
    columns, packed, all_lats = table.shape
    pairs = ROWS // 4
    rows = lats * levs * wire_rows
    return pl.pallas_call(
        spectral_kernel,
        out_shape=jax.ShapeDtypeStruct(field.shape, jnp.bfloat16),
        grid_spec=pltpu.PrefetchScalarGridSpec(
            num_scalar_prefetch=1,
            grid=(pairs,),
            in_specs=[
                pl.BlockSpec(field.shape, lambda p, _: (0, 0, 0, 0)),
                pl.BlockSpec((4, packed, all_lats), lambda p, _: (chunk * pairs + p, 0, 0)),
                pl.BlockSpec(vertical.shape, lambda p, _: (0, 0)),
                pl.BlockSpec(first.shape, lambda p, _: (0, 0)),
                pl.BlockSpec(second.shape, lambda p, _: (0, 0)),
            ],
            out_specs=pl.BlockSpec(field.shape, lambda p, _: (0, 0, 0, 0)),
            scratch_shapes=[
                pltpu.VMEM((rows, LANES), jnp.float32),
                pltpu.VMEM((rows, LANES), jnp.float32),
            ],
        ),
        compiler_params=pltpu.CompilerParams(vmem_limit_bytes=VMEM),
        cost_estimate=pl.CostEstimate(
            flops=4 * ROWS * packed * all_lats * LANES + pairs * 4 * packed * vertical.size,
            bytes_accessed=2 * ROWS * packed * all_lats,
            transcendentals=0,
        ),
        name="spectral_chunk",
    )(lower, field, table, vertical, first, second)


def synthesis_kernel(pieces, parity_ref, *refs):
    field_refs, (table_ref, wind_ref) = refs[:pieces], refs[pieces : pieces + 2]
    out_ref = refs[-1]
    half = LANES // 2
    whole = pl.ds(pl.multiple_of(half * parity_ref[0], half), LANES)
    rest = pl.ds(pl.multiple_of(LANES * (1 - parity_ref[0]), half), half)
    fields = [ref[...].astype(jnp.float32) for ref in field_refs]
    fields = jnp.concatenate([f.reshape(-1, f.shape[-2], LANES) for f in fields], axis=0)
    tiles = [
        fields[:, t * ROWS : (t + 1) * ROWS, :].reshape(-1, LANES).astype(jnp.bfloat16)
        for t in range(6)
    ]
    sums = dot(jnp.concatenate(tiles, axis=1), table_ref[...], ((0,), (0,)))

    def put(t, j, rows, value):
        gain = wind_ref[t, 0, j, rows, :].astype(jnp.float32)
        out_ref[t, 0, j, rows, :] = (value * gain).astype(jnp.bfloat16)

    for j in range(2):
        first = j * 3 * LANES
        for t in range(2):
            put(t, j, whole, sums[first + t * LANES : first + (t + 1) * LANES])
            start = first + 2 * LANES + t * half
            put(t, j, rest, sums[start : start + half])


def synthesis_part(fields, table, wind, parity, first_step, steps, before):
    _, _, _, lat_rows, points = wind.shape
    columns = table.shape[0]
    rows = 6 * ROWS

    def field_spec(array, offset):
        lead = array.ndim - 2
        return pl.BlockSpec(
            array.shape[:-2] + (rows, LANES),
            lambda s, _: (0,) * lead + (s + first_step - offset, 0),
        )

    grid_spec = pl.BlockSpec(
        (2, 1, 2, lat_rows, points), lambda s, _: (0, s + first_step, 0, 0, 0)
    )
    in_specs = [field_spec(*f) for f in fields]
    in_specs += [pl.BlockSpec(table.shape, lambda s, _: (0, 0)), grid_spec]
    operands = [f for f, _ in fields] + [table, wind]
    aliases = {}
    if before is not None:
        in_specs.append(pl.BlockSpec(memory_space=pl.ANY))
        aliases = {1 + len(operands): 0}
        operands.append(before)
    part = 4 * steps * lat_rows * points
    return pl.pallas_call(
        functools.partial(synthesis_kernel, len(fields)),
        out_shape=jax.ShapeDtypeStruct(wind.shape, jnp.bfloat16),
        grid_spec=pltpu.PrefetchScalarGridSpec(
            num_scalar_prefetch=1,
            grid=(steps,),
            in_specs=in_specs,
            out_specs=grid_spec,
        ),
        input_output_aliases=aliases,
        compiler_params=pltpu.CompilerParams(vmem_limit_bytes=VMEM),
        cost_estimate=pl.CostEstimate(
            flops=2 * columns * part, bytes_accessed=4 * part, transcendentals=0
        ),
        name="synthesis_part",
    )(parity, *operands)


def swap_along_z(slots):
    lev_devices = lax.axis_size("lev")
    moved = [slots[0]]
    for kz in range(1, len(slots)):
        pairs = [(b, b ^ (CORES * kz)) for b in range(lev_devices)]
        moved.append(lax.ppermute(slots[kz], "lev", pairs))
    return moved


def exchange_in_plane(x, groups):
    return lax.all_to_all(
        x, ("lat", "lev"), split_axis=0, concat_axis=0, tiled=True, axis_index_groups=groups
    )


def xor_order(x, axis, index):
    size = x.shape[axis]
    bit = 1
    while bit < size:
        split = x.shape[:axis] + (size // (2 * bit), 2, bit) + x.shape[axis + 1 :]
        halves = x.reshape(split)
        halves = jnp.where(index & bit != 0, jnp.flip(halves, axis + 1), halves)
        x = halves.reshape(x.shape)
        bit *= 2
    return x


def pipelined_body(adjoint_grid, wind, legendre, vertical, pair_table, degree_matrix):
    level_rows, lat_rows, points = adjoint_grid.shape
    lats = lax.axis_size("lat")
    levs = lax.axis_size("lev")
    layers = levs // CORES
    plane = lats * CORES
    slots, all_lats, packed = legendre.shape
    matrices, levels, _ = vertical.shape
    chunks = slots // ROWS
    pairs = ROWS // 4
    steps = level_rows // 4
    wire_rows = steps * 6 * ROWS

    lat, lev = lax.axis_index("lat"), lax.axis_index("lev")
    layer = lev // CORES
    parity = (lat % 2).astype(jnp.int32).reshape(1)
    groups = [
        [a * levs + z * CORES + c for a in range(lats) for c in range(CORES)] for z in range(layers)
    ]

    table_pairs = xor_order(pair_table.reshape(lats, layers, CORES, chunks, pairs), 1, layer)
    table_pairs = table_pairs.transpose(3, 1, 0, 2, 4)
    waves = jnp.stack([table_pairs, N - 1 - table_pairs], axis=-1)
    waves = jnp.broadcast_to(waves[..., None], waves.shape + (2,)).reshape(chunks, -1, 1)

    grid = adjoint_grid.reshape(2, steps, 2, lat_rows, points)
    wind = wind.reshape(2, steps, 2, lat_rows, points)
    table = legendre.transpose(0, 2, 1)

    slot_level = jnp.arange(levels, dtype=jnp.int32).reshape(layers, CORES, 2, level_rows // 2)
    slot_level = xor_order(slot_level, 0, layer).transpose(2, 1, 0, 3).reshape(levels)
    order = (slot_level[:, None] == jnp.arange(levels)[None, :]).astype(jnp.bfloat16)
    operators = jnp.einsum("av,gvo->gao", order, vertical, preferred_element_type=jnp.float32)
    operators = jnp.einsum(
        "gao,bo->gab", operators.astype(jnp.bfloat16), order, preferred_element_type=jnp.float32
    )
    operators = operators.astype(jnp.bfloat16).reshape(matrices * levels, levels)

    by_degree = jnp.concatenate([degree_matrix, jnp.broadcast_to(degree_matrix[-1:], (packed,))])
    second = jnp.concatenate([degree_matrix[:1], by_degree[: packed - 1]])
    first = jnp.broadcast_to(by_degree[:, None], (by_degree.shape[0], LANES))
    second = jnp.broadcast_to(second[:, None], (packed, LANES))
    first_pair = (lat * levs + lev) * (slots // 4)
    lower = lax.dynamic_slice(pair_table, (first_pair,), (slots // 4,)).reshape(chunks, pairs)

    returned = []
    for q in range(chunks):
        sent = fourier_chunk(grid, waves[q], parity)
        sent = sent.reshape(layers, plane, wire_rows, LANES)
        moved = swap_along_z([sent[k] for k in range(layers)])
        moved = jnp.stack(moved, axis=1).reshape(plane, layers * wire_rows, LANES)
        field = exchange_in_plane(moved, groups).reshape(lats, levs, wire_rows, LANES)
        field = spectral_chunk(field, table, operators, first, second, lower[q], q)
        moved = exchange_in_plane(field.reshape(plane, layers * wire_rows, LANES), groups)
        returned.append(moved.reshape(plane, layers, wire_rows, LANES))

    synthesis = synthesis_rows(waves.reshape(-1, 1), points, ROWS * layers * plane)
    early = chunks // 2
    fields = []
    for q in range(early):
        fields += swap_along_z([returned[q][:, k] for k in range(layers)])
    out = None
    rows = 6 * ROWS
    parts = steps // 2 if steps % 2 == 0 else 1
    parts = steps if parts == 0 else steps // parts
    for first_step in range(0, steps, parts):
        cut = slice(first_step * rows, (first_step + parts) * rows)
        sent = [jnp.stack([x[:, k, cut] for x in returned[early:]]) for k in range(layers)]
        moved = swap_along_z(sent)
        late = [moved[k][i] for i in range(chunks - early) for k in range(layers)]
        out = synthesis_part(
            [(f, 0) for f in fields] + [(f, first_step) for f in late],
            synthesis,
            wind,
            parity,
            first_step,
            parts,
            out,
        )
    return out.reshape(level_rows, lat_rows, points)


def body(adjoint_grid, wind, legendre, vertical, pair_table, degree_matrix):
    level_rows, lat_rows, points = adjoint_grid.shape
    lats, levs = lax.axis_size("lat"), lax.axis_size("lev")
    layers = levs // CORES
    fits = (
        levs % CORES == 0
        and layers & (layers - 1) == 0
        and lats % 2 == 0
        and lat_rows == LANES + LANES // 2
        and level_rows % 16 == 0
        and vertical.shape[1] == LANES
        and points % LANES == 0
        and points // LANES <= LANES
        and legendre.shape[0] % (2 * ROWS) == 0
        and legendre.shape[2] % 8 == 0
        and legendre.shape[2] > N
        and pair_table.shape[0] * 4 == legendre.shape[0] * lats * levs
    )
    plan = pipelined_body if fits else general_body
    return plan(adjoint_grid, wind, legendre, vertical, pair_table, degree_matrix)


def solution(mesh):
    placed = (
        P("lev", "lat", None),
        P("lev", "lat", None),
        P(("lat", "lev"), None, None),
        P(),
        P(),
        P(),
    )
    return jax.shard_map(
        body, mesh=mesh, in_specs=placed, out_specs=P("lev", "lat", None), check_vma=False
    )
```

```python
import functools
import math

import jax
import jax.numpy as jnp
from jax import lax
from jax.experimental import pallas as pl
from jax.experimental.pallas import tpu as pltpu
from jax.sharding import PartitionSpec as P

N = 512
CORES = 2
ROWS = 8
LANES = 128
VMEM = 48 * 2**20
LONG = pl.CostEstimate(flops=10**13, bytes_accessed=10**8, transcendentals=0)
SHORT = pl.CostEstimate(flops=1, bytes_accessed=1, transcendentals=0)
SIN = (-1.0 / 39916800, 1.0 / 362880, -1.0 / 5040, 1.0 / 120, -1.0 / 6, 1.0)
ANYWHERE = pl.BlockSpec(memory_space=pl.ANY)


def fourier_basis(wavenumbers, points):
    longitude = jnp.arange(points, dtype=jnp.int32)
    phases = wavenumbers[:, :, None] * longitude[None, None, :] % points
    angles = phases.astype(jnp.float32) * (2.0 * jnp.pi / points)
    basis = jnp.stack([jnp.cos(angles), -jnp.sin(angles)], axis=2)
    return basis.reshape(-1, points)


def member_layout(lower_wave, row_total):
    packed_buffer = jnp.arange(row_total, dtype=jnp.int32)
    first_member = packed_buffer[None, :] < (N - lower_wave)[:, None]
    second_member = jnp.logical_not(first_member) & (packed_buffer[None, :] <= N)
    degree = jnp.where(
        first_member, lower_wave[:, None] + packed_buffer[None, :], packed_buffer[None, :] - 1
    )
    degree = jnp.clip(degree, 0, N - 1)
    return (first_member, second_member, degree)


def solve_columns(spectral_state, matrix_index, vertical):

    def add_matrix(operator_index, running):
        product = jnp.einsum(
            "xjm,mg->xjg",
            spectral_state,
            vertical[operator_index],
            preferred_element_type=jnp.float32,
        )
        return running + jnp.where((matrix_index == operator_index)[:, :, None], product, 0.0)

    zero_sums = jnp.zeros(spectral_state.shape, jnp.float32)
    return lax.fori_loop(0, vertical.shape[0], add_matrix, zero_sums).astype(jnp.bfloat16)


def general_body(adjoint_grid, wind, legendre, vertical, pair_table, degree_matrix):
    vertical_level_rows, lat_rows, points = adjoint_grid.shape
    lat_devices = lax.axis_size("lat")
    lev_devices = lax.axis_size("lev")
    slots = legendre.shape[0]
    all_lats = legendre.shape[1]
    packed_rows = legendre.shape[2]
    levels = vertical.shape[1]
    wavenumbers = jnp.stack([pair_table, N - 1 - pair_table], axis=1)
    basis = fourier_basis(wavenumbers, points)
    analysis_table = (basis * (1.0 / math.sqrt(points))).astype(jnp.bfloat16)
    synthesis_table = (basis * (1.0 / math.sqrt(N))).astype(jnp.bfloat16)
    fourier = jnp.einsum(
        "cx,vlx->cvl", analysis_table, adjoint_grid, preferred_element_type=jnp.float32
    )
    fourier = fourier.astype(jnp.bfloat16).reshape(
        lat_devices, lev_devices, slots, vertical_level_rows, lat_rows
    )
    moved = lax.all_to_all(
        lax.all_to_all(fourier, "lev", split_axis=1, concat_axis=3, tiled=True),
        "lat",
        split_axis=0,
        concat_axis=4,
        tiled=True,
    )
    field_stack = moved.reshape(slots, levels, all_lats)
    first_slot = (lax.axis_index("lat") * lev_devices + lax.axis_index("lev")) * slots
    column = first_slot + jnp.arange(slots, dtype=jnp.int32)
    lower_cols = jnp.take(pair_table, column // 4)
    member = column // 2 % 2
    first_member, second_member, degree = member_layout(lower_cols, packed_rows)
    own_rows = jnp.where((member == 0)[:, None], first_member, second_member).astype(jnp.float32)
    spectral_state = jnp.einsum(
        "peq,pae->pqa", legendre, field_stack, preferred_element_type=jnp.float32
    )
    spectral_state = (spectral_state * own_rows[:, :, None]).astype(jnp.bfloat16)
    matrix_index = jnp.take(degree_matrix, degree)
    solved_columns = solve_columns(spectral_state, matrix_index, vertical)
    gridpoint_coefficients = jnp.einsum(
        "ncb,nba->nac", legendre, solved_columns, preferred_element_type=jnp.float32
    )
    gridpoint_coefficients = gridpoint_coefficients.astype(jnp.bfloat16).reshape(
        1, 1, slots, levels, all_lats
    )
    returned = lax.all_to_all(
        lax.all_to_all(gridpoint_coefficients, "lat", split_axis=4, concat_axis=0, tiled=True),
        "lev",
        split_axis=3,
        concat_axis=1,
        tiled=True,
    )
    columns = returned.reshape(lat_devices * lev_devices * slots, vertical_level_rows, lat_rows)
    regridded = jnp.einsum(
        "cvl,cx->vlx", columns, synthesis_table, preferred_element_type=jnp.float32
    )
    return (regridded * wind.astype(jnp.float32)).astype(jnp.bfloat16)


def dot(a, b, dims):
    return lax.dot_general(a, b, (dims, ((), ())), preferred_element_type=jnp.float32)


def cos_turn(steps, points):
    rest = steps - points * jnp.floor(steps * (1.0 / points) + 0.5)
    angle = (points // 4 - jnp.abs(rest)) * (2.0 * math.pi / points)
    square = angle * angle
    total = jnp.full_like(square, SIN[0])
    for c in SIN[1:]:
        total = total * square + c
    return total * angle


def make_table(wave, points, scale):
    rows = wave.shape[0]
    lane = lax.broadcasted_iota(jnp.int32, (rows, LANES), 1).astype(jnp.float32)
    part = lax.broadcasted_iota(jnp.int32, (rows, LANES), 0) % 2
    shift = (part * (points // 4)).astype(jnp.float32)
    waves = jnp.broadcast_to(wave, (rows, LANES)).astype(jnp.float32)
    twice = 2.0 * cos_turn(waves * LANES, points)
    tiles = [cos_turn(waves * (lane + i * LANES) + shift, points) * scale for i in range(2)]
    while len(tiles) < points // LANES:
        tiles.append(twice * tiles[-1] - tiles[-2])
    return jnp.concatenate(tiles, axis=1).astype(jnp.bfloat16)


def fourier_kernel(parity_ref, wave_ref, grid_ref, *refs):
    out_refs, table_ref = refs[:-1], refs[-1]
    points = grid_ref.shape[-1]
    rows = sum(ref.shape[0] for ref in out_refs) * ROWS

    @pl.when(pl.program_id(0) == 0)
    def _():
        block = ROWS * 32

        def fill(i, _):
            at = pl.ds(pl.multiple_of(i * block, block), block)
            table_ref[at, :] = make_table(wave_ref[at, :], points, 1.0 / math.sqrt(points))
            return 0

        lax.fori_loop(0, rows // block, fill, 0)

    half = LANES // 2
    whole = pl.ds(pl.multiple_of(half * parity_ref[0], half), LANES)
    rest = pl.ds(pl.multiple_of(LANES * (1 - parity_ref[0]), half), half)
    lines = []
    for j in range(2):
        lines += [grid_ref[t, 0, j, whole, :] for t in range(2)]
        lines += [grid_ref[t, 0, j, rest, :] for t in range(2)]
    lines = jnp.concatenate(lines, axis=0)
    sums = dot(table_ref[...], lines, ((1,), (1,)))
    sums = sums.reshape(-1, ROWS, sums.shape[1])
    start = 0
    for ref in out_refs:
        part = sums[start : start + ref.shape[0]]
        tiles = [part[:, :, t * LANES : (t + 1) * LANES] for t in range(6)]
        ref[...] = jnp.concatenate(tiles, axis=1).astype(jnp.bfloat16)
        start += ref.shape[0]


def fourier_all(grid, wave, parity, slots):
    _, steps, _, lat_rows, points = grid.shape
    columns = wave.shape[0]
    rows = 6 * ROWS
    return pl.pallas_call(
        fourier_kernel,
        out_shape=[jax.ShapeDtypeStruct((n, steps * rows, LANES), jnp.bfloat16) for n in slots],
        grid_spec=pltpu.PrefetchScalarGridSpec(
            num_scalar_prefetch=1,
            grid=(steps,),
            in_specs=[
                pl.BlockSpec((columns, 1), lambda s, _: (0, 0)),
                pl.BlockSpec((2, 1, 2, lat_rows, points), lambda s, _: (0, s, 0, 0, 0)),
            ],
            out_specs=[pl.BlockSpec((n, rows, LANES), lambda s, _: (0, s, 0)) for n in slots],
            scratch_shapes=[pltpu.VMEM((columns, points), jnp.bfloat16)],
        ),
        compiler_params=pltpu.CompilerParams(vmem_limit_bytes=VMEM),
        cost_estimate=SHORT,
        name="fourier_all",
    )(parity, wave, grid)


def table_kernel(wave_ref, *refs):
    out_ref = refs[-1]
    out_ref[...] = make_table(wave_ref[...], out_ref.shape[1], 1.0 / math.sqrt(N))


def synthesis_rows(wave, points, block, *ready):
    columns = wave.shape[0]
    return pl.pallas_call(
        table_kernel,
        out_shape=jax.ShapeDtypeStruct((columns, points), jnp.bfloat16),
        grid=(columns // block,),
        in_specs=[pl.BlockSpec((block, 1), lambda s: (s, 0))] + [ANYWHERE] * len(ready),
        out_specs=pl.BlockSpec((block, points), lambda s: (s, 0)),
        compiler_params=pltpu.CompilerParams(vmem_limit_bytes=VMEM),
        cost_estimate=LONG,
        name="synthesis_rows",
    )(wave, *ready)


def spectral_kernel(pieces, lower_ref, *refs):
    field_refs = refs[:pieces]
    table_ref, vertical_ref, first_ref, second_ref = refs[pieces : pieces + 4]
    out_ref, field_all, out_all = refs[-3:]
    pair = pl.program_id(0)
    lats, levs, wire_rows, _ = out_ref.shape
    stride = 3 * ROWS
    count = levs * wire_rows // stride
    block = levs * wire_rows
    half = LANES // 2
    packed = table_ref.shape[1]
    couples = vertical_ref.shape[0] // LANES
    middle_row = N // 2

    @pl.when(pair == 0)
    def _():
        plane, rows, _ = field_refs[0].shape
        for i in range(plane):
            for k, ref in enumerate(field_refs):
                start = (i * pieces + k) * rows
                field_all[start : start + rows, :] = ref[i].astype(jnp.float32)

    left = lax.broadcasted_iota(jnp.int32, (count, LANES), 1) < half
    lower = lower_ref[pair]
    row = lax.broadcasted_iota(jnp.int32, (packed, LANES), 0)
    own = row < N - lower
    operator = jnp.where(own, first_ref[pl.ds(lower, packed), :], second_ref[...])
    couple = operator // 2
    odd = operator % 2 == 1
    own = own[middle_row:]
    valid = row[middle_row:] <= N

    def at(lat, t, column):
        return pl.ds(lat * block + t * ROWS + column, count, stride=stride)

    def swap(x):
        return pltpu.roll(x, half, 1)

    def read_field(column):
        tiles = []
        for lat in range(0, lats, 2):
            low = field_all[at(lat, 2, column), :]
            high = field_all[at(lat + 1, 2, column), :]
            middle = [jnp.where(left, low, swap(high)), jnp.where(left, swap(low), high)]
            tiles.append([field_all[at(lat, t, column), :] for t in range(2)])
            tiles.append(middle)
            tiles.append([field_all[at(lat + 1, t, column), :] for t in range(2)])
        levels = [jnp.concatenate([tile[t] for tile in tiles], axis=1) for t in range(2)]
        return jnp.concatenate(levels, axis=0).astype(jnp.bfloat16)

    def write_field(column, value):
        for lat in range(0, lats, 2):
            first = lat // 2 * 3 * LANES
            tile = [value[:, first + i * LANES : first + (i + 1) * LANES] for i in range(3)]
            parts = [[x[:count], x[count:]] for x in tile]
            for t in range(2):
                out_all[at(lat, t, column), :] = parts[0][t]
                out_all[at(lat + 1, t, column), :] = parts[2][t]
            out_all[at(lat, 2, column), :] = jnp.where(left, parts[1][0], swap(parts[1][1]))
            out_all[at(lat + 1, 2, column), :] = jnp.where(left, swap(parts[1][0]), parts[1][1])

    for r in range(2):
        columns = [4 * pair + 2 * e + r for e in range(2)]
        tables = [table_ref.at[r, :N], table_ref.at[2 + r, middle_row:]]
        state = [dot(tables[e][...], read_field(columns[e]), ((1,), (1,))) for e in range(2)]
        upper = jnp.concatenate(
            [state[0][middle_row:], jnp.zeros((packed - N, LANES), jnp.float32)], axis=0
        )
        upper = jnp.where(own, upper, jnp.where(valid, state[1], 0.0))
        spectral = jnp.concatenate([state[0][:middle_row], upper], axis=0)
        spectral = spectral.astype(jnp.bfloat16).astype(jnp.float32)
        spread = [jnp.where(couple == g, spectral, 0.0).astype(jnp.bfloat16) for g in range(couples)]
        solved = dot(jnp.concatenate(spread, axis=1), vertical_ref[...], ((1,), (0,)))
        solved = jnp.where(odd, solved[:, LANES:], solved[:, :LANES])
        upper = solved[middle_row:]
        mine = [
            jnp.concatenate(
                [solved[:middle_row], jnp.where(own, upper, 0.0)[: N - middle_row]], axis=0
            ),
            jnp.where(own, 0.0, upper),
        ]
        for e in range(2):
            value = dot(mine[e].astype(jnp.bfloat16), tables[e][...], ((0,), (0,)))
            write_field(columns[e], value)

    @pl.when(pair == pl.num_programs(0) - 1)
    def _():
        out_ref[...] = out_all[...].astype(jnp.bfloat16).reshape(out_ref.shape)


def spectral_chunk(pieces, table, vertical, first, second, lower, chunk, shape, *ready):
    lats, levs, wire_rows, _ = shape
    columns, packed, all_lats = table.shape
    pairs = ROWS // 4
    rows = lats * levs * wire_rows
    plane = pieces[0].shape[0]
    block = (plane, rows // plane // len(pieces), LANES)
    return pl.pallas_call(
        functools.partial(spectral_kernel, len(pieces)),
        out_shape=jax.ShapeDtypeStruct(shape, jnp.bfloat16),
        grid_spec=pltpu.PrefetchScalarGridSpec(
            num_scalar_prefetch=1,
            grid=(pairs,),
            in_specs=[pl.BlockSpec(block, lambda p, _: (0, 0, 0))] * len(pieces)
            + [
                pl.BlockSpec((4, packed, all_lats), lambda p, _: (chunk * pairs + p, 0, 0)),
                pl.BlockSpec(vertical.shape, lambda p, _: (0, 0)),
                pl.BlockSpec(first.shape, lambda p, _: (0, 0)),
                pl.BlockSpec(second.shape, lambda p, _: (0, 0)),
            ]
            + [ANYWHERE] * len(ready),
            out_specs=pl.BlockSpec(shape, lambda p, _: (0, 0, 0, 0)),
            scratch_shapes=[
                pltpu.VMEM((rows, LANES), jnp.float32),
                pltpu.VMEM((rows, LANES), jnp.float32),
            ],
        ),
        compiler_params=pltpu.CompilerParams(vmem_limit_bytes=VMEM),
        cost_estimate=LONG,
        name="spectral_chunk",
    )(lower, *pieces, table, vertical, first, second, *ready)


def synthesis_kernel(pieces, parity_ref, *refs):
    field_refs, (table_ref, wind_ref) = refs[:pieces], refs[pieces : pieces + 2]
    out_ref = refs[-1]
    half = LANES // 2
    whole = pl.ds(pl.multiple_of(half * parity_ref[0], half), LANES)
    rest = pl.ds(pl.multiple_of(LANES * (1 - parity_ref[0]), half), half)
    fields = [ref[...].astype(jnp.float32) for ref in field_refs]
    fields = jnp.concatenate([f.reshape(-1, f.shape[-2], LANES) for f in fields], axis=0)
    tiles = [
        fields[:, t * ROWS : (t + 1) * ROWS, :].reshape(-1, LANES).astype(jnp.bfloat16)
        for t in range(6)
    ]
    sums = dot(jnp.concatenate(tiles, axis=1), table_ref[...], ((0,), (0,)))

    def put(t, j, rows, value):
        gain = wind_ref[t, 0, j, rows, :].astype(jnp.float32)
        out_ref[t, 0, j, rows, :] = (value * gain).astype(jnp.bfloat16)

    for j in range(2):
        first = j * 3 * LANES
        for t in range(2):
            put(t, j, whole, sums[first + t * LANES : first + (t + 1) * LANES])
            start = first + 2 * LANES + t * half
            put(t, j, rest, sums[start : start + half])


def synthesis_part(fields, table, wind, parity, first_step, steps, before):
    _, _, _, lat_rows, points = wind.shape
    columns = table.shape[0]
    rows = 6 * ROWS

    def field_spec(array, offset):
        lead = array.ndim - 2
        return pl.BlockSpec(
            array.shape[:-2] + (rows, LANES),
            lambda s, _: (0,) * lead + (s + first_step - offset, 0),
        )

    grid_spec = pl.BlockSpec(
        (2, 1, 2, lat_rows, points), lambda s, _: (0, s + first_step, 0, 0, 0)
    )
    in_specs = [field_spec(*f) for f in fields]
    in_specs += [pl.BlockSpec(table.shape, lambda s, _: (0, 0)), grid_spec]
    operands = [f for f, _ in fields] + [table, wind]
    aliases = {}
    if before is not None:
        in_specs.append(ANYWHERE)
        aliases = {1 + len(operands): 0}
        operands.append(before)
    part = 4 * steps * lat_rows * points
    return pl.pallas_call(
        functools.partial(synthesis_kernel, len(fields)),
        out_shape=jax.ShapeDtypeStruct(wind.shape, jnp.bfloat16),
        grid_spec=pltpu.PrefetchScalarGridSpec(
            num_scalar_prefetch=1,
            grid=(steps,),
            in_specs=in_specs,
            out_specs=grid_spec,
        ),
        input_output_aliases=aliases,
        compiler_params=pltpu.CompilerParams(vmem_limit_bytes=VMEM),
        cost_estimate=LONG,
        name="synthesis_part",
    )(parity, *operands)


def after_kernel(*refs):
    del refs


def after(x, *ready):
    return pl.pallas_call(
        after_kernel,
        out_shape=jax.ShapeDtypeStruct(x.shape, x.dtype),
        in_specs=[ANYWHERE] * (1 + len(ready)),
        out_specs=ANYWHERE,
        input_output_aliases={0: 0},
        cost_estimate=LONG,
        name="after",
    )(x, *ready)


def join_kernel(count, *refs):
    out_ref = refs[-1]
    rows = refs[0].shape[1]
    for k in range(count):
        out_ref[:, k * rows : (k + 1) * rows, :] = refs[k][...]


def join_slots(pieces, *ready):
    plane, rows, _ = pieces[0].shape
    all_rows = len(pieces) * rows
    return pl.pallas_call(
        functools.partial(join_kernel, len(pieces)),
        out_shape=jax.ShapeDtypeStruct((plane, all_rows, LANES), jnp.bfloat16),
        grid=(2,),
        in_specs=[pl.BlockSpec((plane // 2, rows, LANES), lambda s: (s, 0, 0))] * len(pieces)
        + [ANYWHERE] * len(ready),
        out_specs=pl.BlockSpec((plane // 2, all_rows, LANES), lambda s: (s, 0, 0)),
        cost_estimate=LONG,
        name="join_slots",
    )(*pieces, *ready)


def part_kernel(layers, parts, *refs):
    in_ref, out_refs = refs[0], refs[len(refs) - parts * (layers - 1) :]
    size = in_ref.shape[1] // layers // parts
    for i, out_ref in enumerate(out_refs):
        p, k = divmod(i, layers - 1)
        start = ((k + 1) * parts + p) * size
        out_ref[...] = in_ref[:, start : start + size, :]


def part_slots(joined, layers, parts, *ready):
    plane, rows, _ = joined.shape
    size = rows // layers // parts
    count = parts * (layers - 1)
    slots = pl.pallas_call(
        functools.partial(part_kernel, layers, parts),
        out_shape=[jax.ShapeDtypeStruct((plane, size, LANES), jnp.bfloat16)] * count,
        grid=(2,),
        in_specs=[pl.BlockSpec((plane // 2, rows, LANES), lambda s: (s, 0, 0))]
        + [ANYWHERE] * len(ready),
        out_specs=[pl.BlockSpec((plane // 2, size, LANES), lambda s: (s, 0, 0))] * count,
        cost_estimate=LONG,
        name="part_slots",
    )(joined, *ready)
    return [slots[p * (layers - 1) : (p + 1) * (layers - 1)] for p in range(parts)]


def swap_along_z(slots):
    lev_devices = lax.axis_size("lev")
    moved = []
    for kz, slot in enumerate(slots, 1):
        pairs = [(b, b ^ (CORES * kz)) for b in range(lev_devices)]
        moved.append(lax.ppermute(slot, "lev", pairs))
    return moved


def exchange_in_plane(x, groups):
    return lax.all_to_all(
        x, ("lat", "lev"), split_axis=0, concat_axis=0, tiled=True, axis_index_groups=groups
    )


def xor_order(x, axis, index):
    size = x.shape[axis]
    bit = 1
    while bit < size:
        split = x.shape[:axis] + (size // (2 * bit), 2, bit) + x.shape[axis + 1 :]
        halves = x.reshape(split)
        halves = jnp.where(index & bit != 0, jnp.flip(halves, axis + 1), halves)
        x = halves.reshape(x.shape)
        bit *= 2
    return x


def pipelined_body(adjoint_grid, wind, legendre, vertical, pair_table, degree_matrix):
    level_rows, lat_rows, points = adjoint_grid.shape
    lats = lax.axis_size("lat")
    levs = lax.axis_size("lev")
    layers = levs // CORES
    plane = lats * CORES
    slots, all_lats, packed = legendre.shape
    matrices, levels, _ = vertical.shape
    chunks = slots // ROWS
    pairs = ROWS // 4
    steps = level_rows // 4
    wire_rows = steps * 6 * ROWS

    lat, lev = lax.axis_index("lat"), lax.axis_index("lev")
    layer = lev // CORES
    parity = (lat % 2).astype(jnp.int32).reshape(1)
    groups = [
        [a * levs + z * CORES + c for a in range(lats) for c in range(CORES)] for z in range(layers)
    ]

    table_pairs = xor_order(pair_table.reshape(lats, layers, CORES, chunks, pairs), 1, layer)
    table_pairs = table_pairs.transpose(3, 1, 0, 2, 4)
    waves = jnp.stack([table_pairs, N - 1 - table_pairs], axis=-1)
    waves = jnp.broadcast_to(waves[..., None], waves.shape + (2,))
    waves = waves.reshape(chunks, layers, plane, ROWS)

    grid = adjoint_grid.reshape(2, steps, 2, lat_rows, points)
    wind = wind.reshape(2, steps, 2, lat_rows, points)
    table = legendre.transpose(0, 2, 1)

    slot_level = jnp.arange(levels, dtype=jnp.int32).reshape(layers, CORES, 2, level_rows // 2)
    slot_level = xor_order(slot_level, 0, layer).transpose(2, 1, 0, 3).reshape(levels)
    order = (slot_level[:, None] == jnp.arange(levels)[None, :]).astype(jnp.bfloat16)
    operators = jnp.einsum("av,gvo->gao", order, vertical, preferred_element_type=jnp.float32)
    operators = jnp.einsum(
        "gao,bo->gab", operators.astype(jnp.bfloat16), order, preferred_element_type=jnp.float32
    )
    operators = operators.astype(jnp.bfloat16).reshape(matrices // 2, 2, levels, levels)
    operators = operators.transpose(0, 2, 1, 3).reshape(matrices // 2 * levels, 2 * levels)

    by_degree = jnp.concatenate([degree_matrix, jnp.broadcast_to(degree_matrix[-1:], (packed,))])
    second = jnp.concatenate([degree_matrix[:1], by_degree[: packed - 1]])
    first = jnp.broadcast_to(by_degree[:, None], (by_degree.shape[0], LANES))
    second = jnp.broadcast_to(second[:, None], (packed, LANES))
    first_pair = (lat * levs + lev) * (slots // 4)
    lower = lax.dynamic_slice(pair_table, (first_pair,), (slots // 4,)).reshape(chunks, pairs)

    joined_shape = (plane, layers * wire_rows, LANES)

    def across(x):
        return exchange_in_plane(x, groups)

    def along(first_slot, slots):
        return [first_slot] + swap_along_z(slots)

    def solve(q, pieces, *ready):
        shape = (lats, levs, wire_rows, LANES)
        x = spectral_chunk(pieces, table, operators, first, second, lower[q], q, shape, *ready)
        return x.reshape(joined_shape)

    rows = [waves[0], waves[1], waves[2].transpose(1, 0, 2), waves[3].transpose(1, 0, 2)]
    rows = jnp.stack([w.reshape(-1) for w in rows]).reshape(-1, 1)
    sent = fourier_all(grid, rows, parity, [plane] * (2 * layers) + [plane * layers] * 2)
    x2, x3 = [x.reshape(joined_shape) for x in sent[2 * layers :]]
    z0 = along(sent[0], sent[1:layers])
    z1 = along(sent[layers], sent[layers + 1 : 2 * layers])
    p2 = across(x2)
    x3 = after(x3, p2)
    p3 = across(x3)
    j0 = join_slots(z0, x3)
    u2 = part_slots(p2, layers, 1, x3)[0]
    z2 = along(p2, u2)
    j1 = join_slots(z1, u2[0])
    j0 = after(j0, p3, j1)
    p0 = across(j0)
    u3 = part_slots(p3, layers, 1, j0)[0]
    z3 = along(p3, u3)
    s0 = solve(0, [p0], u3[0])
    r0 = across(s0)
    s2 = solve(2, z2, s0)
    j1 = after(j1, r0, s2)
    p1 = across(j1)
    b0 = part_slots(r0, layers, 1, j1)[0]
    back0 = along(r0, b0)
    s3 = solve(3, z3, b0[0])
    s2 = after(s2, p1, s3)
    r2 = across(s2)
    s1 = solve(1, [p1], s2)
    s1 = after(s1, r2)
    r1 = across(s1)
    b2 = part_slots(r2, layers, 1, s1)[0]
    back2 = along(r2, b2)
    synthesis = synthesis_rows(waves.reshape(-1, 1), points, ROWS * layers * plane, b2[0])
    s3 = after(s3, r1, synthesis)
    r3 = across(s3)
    b1 = part_slots(r1, layers, 1, s3)[0]
    back1 = along(r1, b1)
    late = [along(r3, part) for part in part_slots(r3, layers, steps, b1[0])]
    fields = back0 + back1 + back2

    out = None
    for step in range(steps):
        out = synthesis_part(
            [(f, 0) for f in fields] + [(late[step][0], 0)] + [(f, step) for f in late[step][1:]],
            synthesis,
            wind,
            parity,
            step,
            1,
            out,
        )
    return out.reshape(level_rows, lat_rows, points)


def body(adjoint_grid, wind, legendre, vertical, pair_table, degree_matrix):
    level_rows, lat_rows, points = adjoint_grid.shape
    lats, levs = lax.axis_size("lat"), lax.axis_size("lev")
    layers = levs // CORES
    fits = (
        levs % CORES == 0
        and layers & (layers - 1) == 0
        and lats % 2 == 0
        and lat_rows == LANES + LANES // 2
        and level_rows % 16 == 0
        and vertical.shape[0] % 2 == 0
        and vertical.shape[1] == LANES
        and points % LANES == 0
        and points // LANES <= LANES
        and legendre.shape[0] % ROWS == 0
        and legendre.shape[0] // ROWS == 4
        and legendre.shape[2] % 8 == 0
        and legendre.shape[2] > N
        and pair_table.shape[0] * 4 == legendre.shape[0] * lats * levs
    )
    plan = pipelined_body if fits else general_body
    return plan(adjoint_grid, wind, legendre, vertical, pair_table, degree_matrix)


def solution(mesh):
    placed = (
        P("lev", "lat", None),
        P("lev", "lat", None),
        P(("lat", "lev"), None, None),
        P(),
        P(),
        P(),
    )
    return jax.shard_map(
        body, mesh=mesh, in_specs=placed, out_specs=P("lev", "lat", None), check_vma=False
    )
```

```python
import functools
import math

import jax
import jax.numpy as jnp
from jax import lax
from jax.experimental import pallas as pl
from jax.experimental.pallas import tpu as pltpu
from jax.sharding import PartitionSpec as P

N = 512
CORES = 2
ROWS = 8
LANES = 128
VMEM = 48 * 2**20
LONG = pl.CostEstimate(flops=10**13, bytes_accessed=10**8, transcendentals=0)
SHORT = pl.CostEstimate(flops=1, bytes_accessed=1, transcendentals=0)
SIN = (-1.0 / 39916800, 1.0 / 362880, -1.0 / 5040, 1.0 / 120, -1.0 / 6, 1.0)
ANYWHERE = pl.BlockSpec(memory_space=pl.ANY)


def fourier_basis(wavenumbers, points):
    longitude = jnp.arange(points, dtype=jnp.int32)
    phases = wavenumbers[:, :, None] * longitude[None, None, :] % points
    angles = phases.astype(jnp.float32) * (2.0 * jnp.pi / points)
    basis = jnp.stack([jnp.cos(angles), -jnp.sin(angles)], axis=2)
    return basis.reshape(-1, points)


def member_layout(lower_wave, row_total):
    packed_buffer = jnp.arange(row_total, dtype=jnp.int32)
    first_member = packed_buffer[None, :] < (N - lower_wave)[:, None]
    second_member = jnp.logical_not(first_member) & (packed_buffer[None, :] <= N)
    degree = jnp.where(
        first_member, lower_wave[:, None] + packed_buffer[None, :], packed_buffer[None, :] - 1
    )
    degree = jnp.clip(degree, 0, N - 1)
    return (first_member, second_member, degree)


def solve_columns(spectral_state, matrix_index, vertical):

    def add_matrix(operator_index, running):
        product = jnp.einsum(
            "xjm,mg->xjg",
            spectral_state,
            vertical[operator_index],
            preferred_element_type=jnp.float32,
        )
        return running + jnp.where((matrix_index == operator_index)[:, :, None], product, 0.0)

    zero_sums = jnp.zeros(spectral_state.shape, jnp.float32)
    return lax.fori_loop(0, vertical.shape[0], add_matrix, zero_sums).astype(jnp.bfloat16)


def general_body(adjoint_grid, wind, legendre, vertical, pair_table, degree_matrix):
    vertical_level_rows, lat_rows, points = adjoint_grid.shape
    lat_devices = lax.axis_size("lat")
    lev_devices = lax.axis_size("lev")
    slots = legendre.shape[0]
    all_lats = legendre.shape[1]
    packed_rows = legendre.shape[2]
    levels = vertical.shape[1]
    wavenumbers = jnp.stack([pair_table, N - 1 - pair_table], axis=1)
    basis = fourier_basis(wavenumbers, points)
    analysis_table = (basis * (1.0 / math.sqrt(points))).astype(jnp.bfloat16)
    synthesis_table = (basis * (1.0 / math.sqrt(N))).astype(jnp.bfloat16)
    fourier = jnp.einsum(
        "cx,vlx->cvl", analysis_table, adjoint_grid, preferred_element_type=jnp.float32
    )
    fourier = fourier.astype(jnp.bfloat16).reshape(
        lat_devices, lev_devices, slots, vertical_level_rows, lat_rows
    )
    moved = lax.all_to_all(
        lax.all_to_all(fourier, "lev", split_axis=1, concat_axis=3, tiled=True),
        "lat",
        split_axis=0,
        concat_axis=4,
        tiled=True,
    )
    field_stack = moved.reshape(slots, levels, all_lats)
    first_slot = (lax.axis_index("lat") * lev_devices + lax.axis_index("lev")) * slots
    column = first_slot + jnp.arange(slots, dtype=jnp.int32)
    lower_cols = jnp.take(pair_table, column // 4)
    member = column // 2 % 2
    first_member, second_member, degree = member_layout(lower_cols, packed_rows)
    own_rows = jnp.where((member == 0)[:, None], first_member, second_member).astype(jnp.float32)
    spectral_state = jnp.einsum(
        "peq,pae->pqa", legendre, field_stack, preferred_element_type=jnp.float32
    )
    spectral_state = (spectral_state * own_rows[:, :, None]).astype(jnp.bfloat16)
    matrix_index = jnp.take(degree_matrix, degree)
    solved_columns = solve_columns(spectral_state, matrix_index, vertical)
    gridpoint_coefficients = jnp.einsum(
        "ncb,nba->nac", legendre, solved_columns, preferred_element_type=jnp.float32
    )
    gridpoint_coefficients = gridpoint_coefficients.astype(jnp.bfloat16).reshape(
        1, 1, slots, levels, all_lats
    )
    returned = lax.all_to_all(
        lax.all_to_all(gridpoint_coefficients, "lat", split_axis=4, concat_axis=0, tiled=True),
        "lev",
        split_axis=3,
        concat_axis=1,
        tiled=True,
    )
    columns = returned.reshape(lat_devices * lev_devices * slots, vertical_level_rows, lat_rows)
    regridded = jnp.einsum(
        "cvl,cx->vlx", columns, synthesis_table, preferred_element_type=jnp.float32
    )
    return (regridded * wind.astype(jnp.float32)).astype(jnp.bfloat16)


def dot(a, b, dims):
    return lax.dot_general(a, b, (dims, ((), ())), preferred_element_type=jnp.float32)


def cos_turn(steps, points):
    rest = steps - points * jnp.floor(steps * (1.0 / points) + 0.5)
    angle = (points // 4 - jnp.abs(rest)) * (2.0 * math.pi / points)
    square = angle * angle
    total = jnp.full_like(square, SIN[0])
    for c in SIN[1:]:
        total = total * square + c
    return total * angle


def make_table(wave, points, scale):
    rows = wave.shape[0]
    lane = lax.broadcasted_iota(jnp.int32, (rows, LANES), 1).astype(jnp.float32)
    part = lax.broadcasted_iota(jnp.int32, (rows, LANES), 0) % 2
    shift = (part * (points // 4)).astype(jnp.float32)
    waves = jnp.broadcast_to(wave, (rows, LANES)).astype(jnp.float32)
    twice = 2.0 * cos_turn(waves * LANES, points)
    tiles = [cos_turn(waves * (lane + i * LANES) + shift, points) * scale for i in range(2)]
    while len(tiles) < points // LANES:
        tiles.append(twice * tiles[-1] - tiles[-2])
    return jnp.concatenate(tiles, axis=1).astype(jnp.bfloat16)


def fourier_kernel(parity_ref, wave_ref, grid_ref, *refs):
    out_refs, table_ref = refs[:-1], refs[-1]
    points = grid_ref.shape[-1]
    rows = sum(ref.shape[0] for ref in out_refs) * ROWS

    @pl.when(pl.program_id(0) == 0)
    def _():
        block = ROWS * 32

        def fill(i, _):
            at = pl.ds(pl.multiple_of(i * block, block), block)
            table_ref[at, :] = make_table(wave_ref[at, :], points, 1.0 / math.sqrt(points))
            return 0

        lax.fori_loop(0, rows // block, fill, 0)

    half = LANES // 2
    whole = pl.ds(pl.multiple_of(half * parity_ref[0], half), LANES)
    rest = pl.ds(pl.multiple_of(LANES * (1 - parity_ref[0]), half), half)
    lines = []
    for j in range(2):
        lines += [grid_ref[t, 0, j, whole, :] for t in range(2)]
        lines += [grid_ref[t, 0, j, rest, :] for t in range(2)]
    lines = jnp.concatenate(lines, axis=0)
    sums = dot(table_ref[...], lines, ((1,), (1,)))
    sums = sums.reshape(-1, ROWS, sums.shape[1])
    start = 0
    for ref in out_refs:
        part = sums[start : start + ref.shape[0]]
        tiles = [part[:, :, t * LANES : (t + 1) * LANES] for t in range(6)]
        ref[...] = jnp.concatenate(tiles, axis=1).astype(jnp.bfloat16)
        start += ref.shape[0]


def fourier_all(grid, wave, parity, slots):
    _, steps, _, lat_rows, points = grid.shape
    columns = wave.shape[0]
    rows = 6 * ROWS
    return pl.pallas_call(
        fourier_kernel,
        out_shape=[jax.ShapeDtypeStruct((n, steps * rows, LANES), jnp.bfloat16) for n in slots],
        grid_spec=pltpu.PrefetchScalarGridSpec(
            num_scalar_prefetch=1,
            grid=(steps,),
            in_specs=[
                pl.BlockSpec((columns, 1), lambda s, _: (0, 0)),
                pl.BlockSpec((2, 1, 2, lat_rows, points), lambda s, _: (0, s, 0, 0, 0)),
            ],
            out_specs=[pl.BlockSpec((n, rows, LANES), lambda s, _: (0, s, 0)) for n in slots],
            scratch_shapes=[pltpu.VMEM((columns, points), jnp.bfloat16)],
        ),
        compiler_params=pltpu.CompilerParams(vmem_limit_bytes=VMEM),
        cost_estimate=SHORT,
        name="fourier_all",
    )(parity, wave, grid)


def table_kernel(wave_ref, *refs):
    out_ref = refs[-1]
    out_ref[...] = make_table(wave_ref[...], out_ref.shape[1], 1.0 / math.sqrt(N))


def synthesis_rows(wave, points, block, *ready):
    columns = wave.shape[0]
    return pl.pallas_call(
        table_kernel,
        out_shape=jax.ShapeDtypeStruct((columns, points), jnp.bfloat16),
        grid=(columns // block,),
        in_specs=[pl.BlockSpec((block, 1), lambda s: (s, 0))] + [ANYWHERE] * len(ready),
        out_specs=pl.BlockSpec((block, points), lambda s: (s, 0)),
        compiler_params=pltpu.CompilerParams(vmem_limit_bytes=VMEM),
        cost_estimate=LONG,
        name="synthesis_rows",
    )(wave, *ready)


def spectral_kernel(pieces, lower_ref, *refs):
    field_refs = refs[:pieces]
    table_ref, vertical_ref, first_ref, second_ref = refs[pieces : pieces + 4]
    out_ref, field_all, out_all = refs[-3:]
    pair = pl.program_id(0)
    lats, levs, wire_rows, _ = out_ref.shape
    stride = 3 * ROWS
    count = levs * wire_rows // stride
    block = levs * wire_rows
    half = LANES // 2
    packed = table_ref.shape[1]
    couples = vertical_ref.shape[0] // LANES
    middle_row = N // 2

    @pl.when(pair == 0)
    def _():
        plane, rows, _ = field_refs[0].shape
        for i in range(plane):
            for k, ref in enumerate(field_refs):
                start = (i * pieces + k) * rows
                field_all[start : start + rows, :] = ref[i].astype(jnp.float32)

    left = lax.broadcasted_iota(jnp.int32, (count, LANES), 1) < half
    lower = lower_ref[pair]
    row = lax.broadcasted_iota(jnp.int32, (packed, LANES), 0)
    own = row < N - lower
    operator = jnp.where(own, first_ref[pl.ds(lower, packed), :], second_ref[...])
    couple = operator // 2
    odd = operator % 2 == 1
    own = own[middle_row:]
    valid = row[middle_row:] <= N

    def at(lat, t, column):
        return pl.ds(lat * block + t * ROWS + column, count, stride=stride)

    def swap(x):
        return pltpu.roll(x, half, 1)

    def read_field(column):
        tiles = []
        for lat in range(0, lats, 2):
            low = field_all[at(lat, 2, column), :]
            high = field_all[at(lat + 1, 2, column), :]
            middle = [jnp.where(left, low, swap(high)), jnp.where(left, swap(low), high)]
            tiles.append([field_all[at(lat, t, column), :] for t in range(2)])
            tiles.append(middle)
            tiles.append([field_all[at(lat + 1, t, column), :] for t in range(2)])
        levels = [jnp.concatenate([tile[t] for tile in tiles], axis=1) for t in range(2)]
        return jnp.concatenate(levels, axis=0).astype(jnp.bfloat16)

    def write_field(column, value):
        for lat in range(0, lats, 2):
            first = lat // 2 * 3 * LANES
            tile = [value[:, first + i * LANES : first + (i + 1) * LANES] for i in range(3)]
            parts = [[x[:count], x[count:]] for x in tile]
            for t in range(2):
                out_all[at(lat, t, column), :] = parts[0][t]
                out_all[at(lat + 1, t, column), :] = parts[2][t]
            out_all[at(lat, 2, column), :] = jnp.where(left, parts[1][0], swap(parts[1][1]))
            out_all[at(lat + 1, 2, column), :] = jnp.where(left, swap(parts[1][0]), parts[1][1])

    for r in range(2):
        columns = [4 * pair + 2 * e + r for e in range(2)]
        tables = [table_ref.at[r, :N], table_ref.at[2 + r, middle_row:]]
        state = [dot(tables[e][...], read_field(columns[e]), ((1,), (1,))) for e in range(2)]
        upper = jnp.concatenate(
            [state[0][middle_row:], jnp.zeros((packed - N, LANES), jnp.float32)], axis=0
        )
        upper = jnp.where(own, upper, jnp.where(valid, state[1], 0.0))
        spectral = jnp.concatenate([state[0][:middle_row], upper], axis=0)
        spectral = spectral.astype(jnp.bfloat16).astype(jnp.float32)
        spread = [jnp.where(couple == g, spectral, 0.0).astype(jnp.bfloat16) for g in range(couples)]
        solved = dot(jnp.concatenate(spread, axis=1), vertical_ref[...], ((1,), (0,)))
        solved = jnp.where(odd, solved[:, LANES:], solved[:, :LANES])
        upper = solved[middle_row:]
        mine = [
            jnp.concatenate(
                [solved[:middle_row], jnp.where(own, upper, 0.0)[: N - middle_row]], axis=0
            ),
            jnp.where(own, 0.0, upper),
        ]
        for e in range(2):
            value = dot(mine[e].astype(jnp.bfloat16), tables[e][...], ((0,), (0,)))
            write_field(columns[e], value)

    @pl.when(pair == pl.num_programs(0) - 1)
    def _():
        out_ref[...] = out_all[...].astype(jnp.bfloat16).reshape(out_ref.shape)


def spectral_chunk(pieces, table, vertical, first, second, lower, chunk, shape, *ready):
    lats, levs, wire_rows, _ = shape
    columns, packed, all_lats = table.shape
    pairs = ROWS // 4
    rows = lats * levs * wire_rows
    plane = pieces[0].shape[0]
    block = (plane, rows // plane // len(pieces), LANES)
    return pl.pallas_call(
        functools.partial(spectral_kernel, len(pieces)),
        out_shape=jax.ShapeDtypeStruct(shape, jnp.bfloat16),
        grid_spec=pltpu.PrefetchScalarGridSpec(
            num_scalar_prefetch=1,
            grid=(pairs,),
            in_specs=[pl.BlockSpec(block, lambda p, _: (0, 0, 0))] * len(pieces)
            + [
                pl.BlockSpec((4, packed, all_lats), lambda p, _: (chunk * pairs + p, 0, 0)),
                pl.BlockSpec(vertical.shape, lambda p, _: (0, 0)),
                pl.BlockSpec(first.shape, lambda p, _: (0, 0)),
                pl.BlockSpec(second.shape, lambda p, _: (0, 0)),
            ]
            + [ANYWHERE] * len(ready),
            out_specs=pl.BlockSpec(shape, lambda p, _: (0, 0, 0, 0)),
            scratch_shapes=[
                pltpu.VMEM((rows, LANES), jnp.float32),
                pltpu.VMEM((rows, LANES), jnp.float32),
            ],
        ),
        compiler_params=pltpu.CompilerParams(vmem_limit_bytes=VMEM),
        cost_estimate=LONG,
        name="spectral_chunk",
    )(lower, *pieces, table, vertical, first, second, *ready)


def synthesis_kernel(pieces, parity_ref, *refs):
    field_refs, (table_ref, wind_ref) = refs[:pieces], refs[pieces : pieces + 2]
    out_ref, lines_ref = refs[-2:]
    half = LANES // 2
    whole = pl.ds(pl.multiple_of(half * parity_ref[0], half), LANES)
    rest = pl.ds(pl.multiple_of(LANES * (1 - parity_ref[0]), half), half)

    fields = [ref[...].astype(jnp.float32) for ref in field_refs]
    fields = jnp.concatenate(fields, axis=0)
    for t in range(6):
        tile = fields[:, t * ROWS : (t + 1) * ROWS, :].reshape(-1, LANES)
        lines_ref[t * LANES : (t + 1) * LANES, :] = tile.astype(jnp.bfloat16).T

    sums = dot(lines_ref[...], table_ref[...], ((1,), (0,)))

    def put(t, j, rows, value):
        gain = wind_ref[t, 0, j, rows, :].astype(jnp.float32)
        out_ref[t, 0, j, rows, :] = (value * gain).astype(jnp.bfloat16)

    for j in range(2):
        first = j * 3 * LANES
        for t in range(2):
            put(t, j, whole, sums[first + t * LANES : first + (t + 1) * LANES])
            start = first + 2 * LANES + t * half
            put(t, j, rest, sums[start : start + half])


def synthesis_part(fields, table, wind, parity, start, count, before):
    _, _, _, lat_rows, points = wind.shape
    columns = table.shape[0]
    rows = 6 * ROWS

    def field_spec(array, first):
        return pl.BlockSpec((array.shape[0], rows, LANES), lambda s, _: (0, first + s, 0))

    grid_spec = pl.BlockSpec(
        (2, 1, 2, lat_rows, points), lambda s, _: (0, start + s, 0, 0, 0)
    )
    in_specs = [field_spec(*f) for f in fields]
    in_specs += [pl.BlockSpec((columns, points), lambda s, _: (0, 0)), grid_spec]
    operands = [f for f, _ in fields] + [table, wind]
    aliases = {}
    if before is not None:
        in_specs.append(ANYWHERE)
        aliases = {1 + len(operands): 0}
        operands.append(before)
    return pl.pallas_call(
        functools.partial(synthesis_kernel, len(fields)),
        out_shape=jax.ShapeDtypeStruct(wind.shape, jnp.bfloat16),
        grid_spec=pltpu.PrefetchScalarGridSpec(
            num_scalar_prefetch=1,
            grid=(count,),
            in_specs=in_specs,
            out_specs=grid_spec,
            scratch_shapes=[pltpu.VMEM((6 * LANES, columns), jnp.bfloat16)],
        ),
        input_output_aliases=aliases,
        compiler_params=pltpu.CompilerParams(vmem_limit_bytes=VMEM),
        cost_estimate=LONG,
        name="synthesis_part",
    )(parity, *operands)


def after_kernel(*refs):
    del refs


def after(x, *ready):
    return pl.pallas_call(
        after_kernel,
        out_shape=jax.ShapeDtypeStruct(x.shape, x.dtype),
        in_specs=[ANYWHERE] * (1 + len(ready)),
        out_specs=ANYWHERE,
        input_output_aliases={0: 0},
        cost_estimate=LONG,
        name="after",
    )(x, *ready)


def join_kernel(count, *refs):
    out_ref = refs[-1]
    rows = refs[0].shape[1]
    for k in range(count):
        out_ref[:, k * rows : (k + 1) * rows, :] = refs[k][...]


def join_slots(pieces, *ready):
    plane, rows, _ = pieces[0].shape
    all_rows = len(pieces) * rows
    return pl.pallas_call(
        functools.partial(join_kernel, len(pieces)),
        out_shape=jax.ShapeDtypeStruct((plane, all_rows, LANES), jnp.bfloat16),
        grid=(2,),
        in_specs=[pl.BlockSpec((plane // 2, rows, LANES), lambda s: (s, 0, 0))] * len(pieces)
        + [ANYWHERE] * len(ready),
        out_specs=pl.BlockSpec((plane // 2, all_rows, LANES), lambda s: (s, 0, 0)),
        cost_estimate=LONG,
        name="join_slots",
    )(*pieces, *ready)


def part_kernel(layers, parts, *refs):
    in_ref, out_refs = refs[0], refs[len(refs) - parts * (layers - 1) :]
    size = in_ref.shape[1] // layers // parts
    for i, out_ref in enumerate(out_refs):
        p, k = divmod(i, layers - 1)
        start = ((k + 1) * parts + p) * size
        out_ref[...] = in_ref[:, start : start + size, :]


def part_slots(joined, layers, parts, *ready):
    plane, rows, _ = joined.shape
    size = rows // layers // parts
    count = parts * (layers - 1)
    slots = pl.pallas_call(
        functools.partial(part_kernel, layers, parts),
        out_shape=[jax.ShapeDtypeStruct((plane, size, LANES), jnp.bfloat16)] * count,
        grid=(2,),
        in_specs=[pl.BlockSpec((plane // 2, rows, LANES), lambda s: (s, 0, 0))]
        + [ANYWHERE] * len(ready),
        out_specs=[pl.BlockSpec((plane // 2, size, LANES), lambda s: (s, 0, 0))] * count,
        cost_estimate=LONG,
        name="part_slots",
    )(joined, *ready)
    return [slots[p * (layers - 1) : (p + 1) * (layers - 1)] for p in range(parts)]


def turn_along_z(slots, sign):
    lev_devices = lax.axis_size("lev")
    moved = []
    for k, slot in enumerate(slots, 1):
        pairs = [(b, (b + sign * CORES * k) % lev_devices) for b in range(lev_devices)]
        moved.append(lax.ppermute(slot, "lev", pairs))
    return moved


def exchange_in_plane(x, groups):
    return lax.all_to_all(
        x, ("lat", "lev"), split_axis=0, concat_axis=0, tiled=True, axis_index_groups=groups
    )


def turned(x, axis, start):
    size = x.shape[axis]
    return lax.dynamic_slice_in_dim(jnp.concatenate([x, x], axis=axis), start, size, axis)


def pipelined_body(adjoint_grid, wind, legendre, vertical, pair_table, degree_matrix):
    level_rows, lat_rows, points = adjoint_grid.shape
    lats = lax.axis_size("lat")
    levs = lax.axis_size("lev")
    layers = levs // CORES
    plane = lats * CORES
    slots, all_lats, packed = legendre.shape
    matrices, levels, _ = vertical.shape
    chunks = slots // ROWS
    pairs = ROWS // 4
    steps = level_rows // 4
    wire_rows = steps * 6 * ROWS

    lat, lev = lax.axis_index("lat"), lax.axis_index("lev")
    layer = lev // CORES
    parity = (lat % 2).astype(jnp.int32).reshape(1)
    groups = [
        [a * levs + z * CORES + c for a in range(lats) for c in range(CORES)] for z in range(layers)
    ]

    table_pairs = turned(pair_table.reshape(lats, layers, CORES, chunks, pairs), 1, layer)
    table_pairs = table_pairs.transpose(3, 1, 0, 2, 4)
    waves = jnp.stack([table_pairs, N - 1 - table_pairs], axis=-1)
    waves = jnp.broadcast_to(waves[..., None], waves.shape + (2,))
    waves = waves.reshape(chunks, layers, plane, ROWS)

    grid = adjoint_grid.reshape(2, steps, 2, lat_rows, points)
    wind = wind.reshape(2, steps, 2, lat_rows, points)
    table = legendre.transpose(0, 2, 1)

    slot_level = jnp.arange(levels, dtype=jnp.int32).reshape(layers, CORES, 2, level_rows // 2)
    slot_level = turned(jnp.flip(slot_level, 0), 0, layers - 1 - layer)
    slot_level = slot_level.transpose(2, 1, 0, 3).reshape(levels)
    order = (slot_level[:, None] == jnp.arange(levels)[None, :]).astype(jnp.bfloat16)
    operators = jnp.einsum("av,gvo->gao", order, vertical, preferred_element_type=jnp.float32)
    operators = jnp.einsum(
        "gao,bo->gab", operators.astype(jnp.bfloat16), order, preferred_element_type=jnp.float32
    )
    operators = operators.astype(jnp.bfloat16).reshape(matrices // 2, 2, levels, levels)
    operators = operators.transpose(0, 2, 1, 3).reshape(matrices // 2 * levels, 2 * levels)

    by_degree = jnp.concatenate([degree_matrix, jnp.broadcast_to(degree_matrix[-1:], (packed,))])
    second = jnp.concatenate([degree_matrix[:1], by_degree[: packed - 1]])
    first = jnp.broadcast_to(by_degree[:, None], (by_degree.shape[0], LANES))
    second = jnp.broadcast_to(second[:, None], (packed, LANES))
    first_pair = (lat * levs + lev) * (slots // 4)
    lower = lax.dynamic_slice(pair_table, (first_pair,), (slots // 4,)).reshape(chunks, pairs)

    parts = 2 if steps % 2 == 0 else 1
    joined_shape = (plane, layers * wire_rows, LANES)

    def across(x):
        return exchange_in_plane(x, groups)

    def along(first_slot, slots):
        return [first_slot] + turn_along_z(slots, 1)

    def home(first_slot, slots):
        return [first_slot] + turn_along_z(slots, -1)

    def solve(q, pieces, *ready):
        shape = (lats, levs, wire_rows, LANES)
        x = spectral_chunk(pieces, table, operators, first, second, lower[q], q, shape, *ready)
        return x.reshape(joined_shape)

    rows = [waves[0], waves[1], waves[2].transpose(1, 0, 2), waves[3].transpose(1, 0, 2)]
    rows = jnp.stack([w.reshape(-1) for w in rows]).reshape(-1, 1)
    sent = fourier_all(grid, rows, parity, [plane] * (2 * layers) + [plane * layers] * 2)
    x2, x3 = [x.reshape(joined_shape) for x in sent[2 * layers :]]
    z0 = along(sent[0], sent[1:layers])
    p2 = across(x2)
    rows = jnp.stack([waves[0], waves[2], waves[3], waves[1]]).reshape(-1, 1)
    synthesis = synthesis_rows(rows, points, ROWS * layers * plane, x2)
    x3 = after(x3, p2, synthesis)
    p3 = across(x3)
    z1 = along(sent[layers], [after(x, x3) for x in sent[layers + 1 : 2 * layers]])
    j0 = after(join_slots(z0, x3), p3)
    p0 = across(j0)
    u2 = part_slots(p2, layers, 1, j0)[0]
    z2 = along(p2, u2)
    s0 = solve(0, [p0], u2[0])
    r0 = across(s0)
    j1 = join_slots(z1, s0)
    u3 = part_slots(p3, layers, 1, j1)[0]
    z3 = along(p3, u3)
    j1 = after(j1, r0, u3[0])
    p1 = across(j1)
    b0 = part_slots(r0, layers, 1, j1)[0]
    back0 = home(r0, b0)
    s2 = after(solve(2, z2, b0[0]), p1)
    r2 = across(s2)
    s3 = after(solve(3, z3, s2), r2)
    r3 = across(s3)
    b2 = part_slots(r2, layers, 1, s3)[0]
    back2 = home(r2, b2)
    s1 = after(solve(1, [p1], b2[0]), r3)
    r1 = across(s1)
    b3 = part_slots(r3, layers, 1, s1)[0]
    back3 = home(r3, b3)
    late = [home(r1, part) for part in part_slots(r1, layers, parts, b3[0])]
    fields = back0 + back2 + back3

    out = None
    for i in range(parts):
        first = i * (steps // parts)
        here = [(f, first) for f in fields] + [(late[i][0], first)]
        here += [(f, 0) for f in late[i][1:]]
        out = synthesis_part(here, synthesis, wind, parity, first, steps // parts, out)
    return out.reshape(level_rows, lat_rows, points)


def body(adjoint_grid, wind, legendre, vertical, pair_table, degree_matrix):
    level_rows, lat_rows, points = adjoint_grid.shape
    lats, levs = lax.axis_size("lat"), lax.axis_size("lev")
    layers = levs // CORES
    fits = (
        levs % CORES == 0
        and lats % 2 == 0
        and lat_rows == LANES + LANES // 2
        and level_rows % 16 == 0
        and vertical.shape[0] % 2 == 0
        and vertical.shape[1] == LANES
        and points % LANES == 0
        and points // LANES <= LANES
        and legendre.shape[0] % ROWS == 0
        and legendre.shape[0] // ROWS == 4
        and legendre.shape[2] % 8 == 0
        and legendre.shape[2] > N
        and pair_table.shape[0] * 4 == legendre.shape[0] * lats * levs
    )
    plan = pipelined_body if fits else general_body
    return plan(adjoint_grid, wind, legendre, vertical, pair_table, degree_matrix)


def solution(mesh):
    placed = (
        P("lev", "lat", None),
        P("lev", "lat", None),
        P(("lat", "lev"), None, None),
        P(),
        P(),
        P(),
    )
    return jax.shard_map(
        body, mesh=mesh, in_specs=placed, out_specs=P("lev", "lat", None), check_vma=False
    )
```

```python
import functools
import math

import jax
import jax.numpy as jnp
from jax import lax
from jax.experimental import pallas as pl
from jax.experimental.pallas import tpu as pltpu
from jax.sharding import PartitionSpec as P

N = 512
CORES = 2
ROWS = 8
LANES = 128
VMEM = 48 * 2**20
LONG = pl.CostEstimate(flops=10**13, bytes_accessed=10**8, transcendentals=0)
SIN = (-1.0 / 39916800, 1.0 / 362880, -1.0 / 5040, 1.0 / 120, -1.0 / 6, 1.0)
ANYWHERE = pl.BlockSpec(memory_space=pl.ANY)


def fourier_basis(wavenumbers, points):
    longitude = jnp.arange(points, dtype=jnp.int32)
    phases = wavenumbers[:, :, None] * longitude[None, None, :] % points
    angles = phases.astype(jnp.float32) * (2.0 * jnp.pi / points)
    basis = jnp.stack([jnp.cos(angles), -jnp.sin(angles)], axis=2)
    return basis.reshape(-1, points)


def member_layout(lower_wave, row_total):
    packed_buffer = jnp.arange(row_total, dtype=jnp.int32)
    first_member = packed_buffer[None, :] < (N - lower_wave)[:, None]
    second_member = jnp.logical_not(first_member) & (packed_buffer[None, :] <= N)
    degree = jnp.where(
        first_member, lower_wave[:, None] + packed_buffer[None, :], packed_buffer[None, :] - 1
    )
    degree = jnp.clip(degree, 0, N - 1)
    return (first_member, second_member, degree)


def solve_columns(spectral_state, matrix_index, vertical):

    def add_matrix(operator_index, running):
        product = jnp.einsum(
            "xjm,mg->xjg",
            spectral_state,
            vertical[operator_index],
            preferred_element_type=jnp.float32,
        )
        return running + jnp.where((matrix_index == operator_index)[:, :, None], product, 0.0)

    zero_sums = jnp.zeros(spectral_state.shape, jnp.float32)
    return lax.fori_loop(0, vertical.shape[0], add_matrix, zero_sums).astype(jnp.bfloat16)


def general_body(adjoint_grid, wind, legendre, vertical, pair_table, degree_matrix):
    vertical_level_rows, lat_rows, points = adjoint_grid.shape
    lat_devices = lax.axis_size("lat")
    lev_devices = lax.axis_size("lev")
    slots = legendre.shape[0]
    all_lats = legendre.shape[1]
    packed_rows = legendre.shape[2]
    levels = vertical.shape[1]
    wavenumbers = jnp.stack([pair_table, N - 1 - pair_table], axis=1)
    basis = fourier_basis(wavenumbers, points)
    analysis_table = (basis * (1.0 / math.sqrt(points))).astype(jnp.bfloat16)
    synthesis_table = (basis * (1.0 / math.sqrt(N))).astype(jnp.bfloat16)
    fourier = jnp.einsum(
        "cx,vlx->cvl", analysis_table, adjoint_grid, preferred_element_type=jnp.float32
    )
    fourier = fourier.astype(jnp.bfloat16).reshape(
        lat_devices, lev_devices, slots, vertical_level_rows, lat_rows
    )
    moved = lax.all_to_all(
        lax.all_to_all(fourier, "lev", split_axis=1, concat_axis=3, tiled=True),
        "lat",
        split_axis=0,
        concat_axis=4,
        tiled=True,
    )
    field_stack = moved.reshape(slots, levels, all_lats)
    first_slot = (lax.axis_index("lat") * lev_devices + lax.axis_index("lev")) * slots
    column = first_slot + jnp.arange(slots, dtype=jnp.int32)
    lower_cols = jnp.take(pair_table, column // 4)
    member = column // 2 % 2
    first_member, second_member, degree = member_layout(lower_cols, packed_rows)
    own_rows = jnp.where((member == 0)[:, None], first_member, second_member).astype(jnp.float32)
    spectral_state = jnp.einsum(
        "peq,pae->pqa", legendre, field_stack, preferred_element_type=jnp.float32
    )
    spectral_state = (spectral_state * own_rows[:, :, None]).astype(jnp.bfloat16)
    matrix_index = jnp.take(degree_matrix, degree)
    solved_columns = solve_columns(spectral_state, matrix_index, vertical)
    gridpoint_coefficients = jnp.einsum(
        "ncb,nba->nac", legendre, solved_columns, preferred_element_type=jnp.float32
    )
    gridpoint_coefficients = gridpoint_coefficients.astype(jnp.bfloat16).reshape(
        1, 1, slots, levels, all_lats
    )
    returned = lax.all_to_all(
        lax.all_to_all(gridpoint_coefficients, "lat", split_axis=4, concat_axis=0, tiled=True),
        "lev",
        split_axis=3,
        concat_axis=1,
        tiled=True,
    )
    columns = returned.reshape(lat_devices * lev_devices * slots, vertical_level_rows, lat_rows)
    regridded = jnp.einsum(
        "cvl,cx->vlx", columns, synthesis_table, preferred_element_type=jnp.float32
    )
    return (regridded * wind.astype(jnp.float32)).astype(jnp.bfloat16)


def dot(a, b, dims):
    return lax.dot_general(a, b, (dims, ((), ())), preferred_element_type=jnp.float32)


def cos_turn(steps, points):
    rest = steps - points * jnp.floor(steps * (1.0 / points) + 0.5)
    angle = (points // 4 - jnp.abs(rest)) * (2.0 * math.pi / points)
    square = angle * angle
    total = jnp.full_like(square, SIN[0])
    for c in SIN[1:]:
        total = total * square + c
    return total * angle


def make_table(wave, points, scale):
    rows = wave.shape[0]
    lane = lax.broadcasted_iota(jnp.int32, (rows, LANES), 1).astype(jnp.float32)
    part = lax.broadcasted_iota(jnp.int32, (rows, LANES), 0) % 2
    shift = (part * (points // 4)).astype(jnp.float32)
    waves = jnp.broadcast_to(wave, (rows, LANES)).astype(jnp.float32)
    twice = 2.0 * cos_turn(waves * LANES, points)
    tiles = [cos_turn(waves * (lane + i * LANES) + shift, points) * scale for i in range(2)]
    while len(tiles) < points // LANES:
        tiles.append(twice * tiles[-1] - tiles[-2])
    return jnp.concatenate(tiles, axis=1).astype(jnp.bfloat16)


def fourier_kernel(waits, parity_ref, wave_ref, grid_ref, *refs):
    out_refs, table_ref = refs[waits:-1], refs[-1]
    points = grid_ref.shape[-1]
    rows = sum(ref.shape[0] for ref in out_refs) * ROWS

    @pl.when(pl.program_id(0) == 0)
    def _():
        block = ROWS * 32

        def fill(i, _):
            at = pl.ds(pl.multiple_of(i * block, block), block)
            table_ref[at, :] = make_table(wave_ref[at, :], points, 1.0 / math.sqrt(points))
            return 0

        lax.fori_loop(0, rows // block, fill, 0)

    half = LANES // 2
    whole = pl.ds(pl.multiple_of(half * parity_ref[0], half), LANES)
    rest = pl.ds(pl.multiple_of(LANES * (1 - parity_ref[0]), half), half)
    lines = []
    for j in range(2):
        lines += [grid_ref[t, 0, j, whole, :] for t in range(2)]
        lines += [grid_ref[t, 0, j, rest, :] for t in range(2)]
    lines = jnp.concatenate(lines, axis=0)
    sums = dot(table_ref[...], lines, ((1,), (1,)))
    sums = sums.reshape(-1, ROWS, sums.shape[1])
    start = 0
    for ref in out_refs:
        part = sums[start : start + ref.shape[0]]
        tiles = [part[:, :, t * LANES : (t + 1) * LANES] for t in range(6)]
        ref[...] = jnp.concatenate(tiles, axis=1).astype(jnp.bfloat16)
        start += ref.shape[0]


def fourier_some(grid, wave, parity, slots, *ready):
    _, steps, _, lat_rows, points = grid.shape
    columns = wave.shape[0]
    rows = 6 * ROWS
    return pl.pallas_call(
        functools.partial(fourier_kernel, len(ready)),
        out_shape=[jax.ShapeDtypeStruct((n, steps * rows, LANES), jnp.bfloat16) for n in slots],
        grid_spec=pltpu.PrefetchScalarGridSpec(
            num_scalar_prefetch=1,
            grid=(steps,),
            in_specs=[
                pl.BlockSpec((columns, 1), lambda s, _: (0, 0)),
                pl.BlockSpec((2, 1, 2, lat_rows, points), lambda s, _: (0, s, 0, 0, 0)),
            ]
            + [ANYWHERE] * len(ready),
            out_specs=[pl.BlockSpec((n, rows, LANES), lambda s, _: (0, s, 0)) for n in slots],
            scratch_shapes=[pltpu.VMEM((columns, points), jnp.bfloat16)],
        ),
        compiler_params=pltpu.CompilerParams(vmem_limit_bytes=VMEM),
        cost_estimate=LONG,
        name="fourier_some",
    )(parity, wave, grid, *ready)


def table_kernel(wave_ref, *refs):
    out_ref = refs[-1]
    out_ref[...] = make_table(wave_ref[...], out_ref.shape[1], 1.0 / math.sqrt(N))


def synthesis_rows(wave, points, block, *ready):
    columns = wave.shape[0]
    return pl.pallas_call(
        table_kernel,
        out_shape=jax.ShapeDtypeStruct((columns, points), jnp.bfloat16),
        grid=(columns // block,),
        in_specs=[pl.BlockSpec((block, 1), lambda s: (s, 0))] + [ANYWHERE] * len(ready),
        out_specs=pl.BlockSpec((block, points), lambda s: (s, 0)),
        compiler_params=pltpu.CompilerParams(vmem_limit_bytes=VMEM),
        cost_estimate=LONG,
        name="synthesis_rows",
    )(wave, *ready)


def spectral_kernel(pieces, lower_ref, *refs):
    field_refs = refs[:pieces]
    table_ref, vertical_ref, first_ref, second_ref = refs[pieces : pieces + 4]
    out_ref, field_all, out_all = refs[-3:]
    pair = pl.program_id(0)
    lats, levs, wire_rows, _ = out_ref.shape
    stride = 3 * ROWS
    count = levs * wire_rows // stride
    block = levs * wire_rows
    half = LANES // 2
    packed = table_ref.shape[1]
    couples = vertical_ref.shape[0] // LANES
    middle_row = N // 2

    @pl.when(pair == 0)
    def _():
        plane, rows, _ = field_refs[0].shape
        for i in range(plane):
            for k, ref in enumerate(field_refs):
                start = (i * pieces + k) * rows
                field_all[start : start + rows, :] = ref[i].astype(jnp.float32)

    left = lax.broadcasted_iota(jnp.int32, (count, LANES), 1) < half
    lower = lower_ref[pair]
    row = lax.broadcasted_iota(jnp.int32, (packed, LANES), 0)
    own = row < N - lower
    operator = jnp.where(own, first_ref[pl.ds(lower, packed), :], second_ref[...])
    couple = operator // 2
    odd = operator % 2 == 1
    own = own[middle_row:]
    valid = row[middle_row:] <= N

    def at(lat, t, column):
        return pl.ds(lat * block + t * ROWS + column, count, stride=stride)

    def swap(x):
        return pltpu.roll(x, half, 1)

    def read_field(column):
        tiles = []
        for lat in range(0, lats, 2):
            low = field_all[at(lat, 2, column), :]
            high = field_all[at(lat + 1, 2, column), :]
            middle = [jnp.where(left, low, swap(high)), jnp.where(left, swap(low), high)]
            tiles.append([field_all[at(lat, t, column), :] for t in range(2)])
            tiles.append(middle)
            tiles.append([field_all[at(lat + 1, t, column), :] for t in range(2)])
        levels = [jnp.concatenate([tile[t] for tile in tiles], axis=1) for t in range(2)]
        return jnp.concatenate(levels, axis=0).astype(jnp.bfloat16)

    def write_field(column, value):
        for lat in range(0, lats, 2):
            first = lat // 2 * 3 * LANES
            tile = [value[:, first + i * LANES : first + (i + 1) * LANES] for i in range(3)]
            parts = [[x[:count], x[count:]] for x in tile]
            for t in range(2):
                out_all[at(lat, t, column), :] = parts[0][t]
                out_all[at(lat + 1, t, column), :] = parts[2][t]
            out_all[at(lat, 2, column), :] = jnp.where(left, parts[1][0], swap(parts[1][1]))
            out_all[at(lat + 1, 2, column), :] = jnp.where(left, swap(parts[1][0]), parts[1][1])

    for r in range(2):
        columns = [4 * pair + 2 * e + r for e in range(2)]
        tables = [table_ref.at[r, :N], table_ref.at[2 + r, middle_row:]]
        state = [dot(tables[e][...], read_field(columns[e]), ((1,), (1,))) for e in range(2)]
        upper = jnp.concatenate(
            [state[0][middle_row:], jnp.zeros((packed - N, LANES), jnp.float32)], axis=0
        )
        upper = jnp.where(own, upper, jnp.where(valid, state[1], 0.0))
        spectral = jnp.concatenate([state[0][:middle_row], upper], axis=0)
        spectral = spectral.astype(jnp.bfloat16).astype(jnp.float32)
        spread = [jnp.where(couple == g, spectral, 0.0).astype(jnp.bfloat16) for g in range(couples)]
        solved = dot(jnp.concatenate(spread, axis=1), vertical_ref[...], ((1,), (0,)))
        solved = jnp.where(odd, solved[:, LANES:], solved[:, :LANES])
        upper = solved[middle_row:]
        mine = [
            jnp.concatenate(
                [solved[:middle_row], jnp.where(own, upper, 0.0)[: N - middle_row]], axis=0
            ),
            jnp.where(own, 0.0, upper),
        ]
        for e in range(2):
            value = dot(mine[e].astype(jnp.bfloat16), tables[e][...], ((0,), (0,)))
            write_field(columns[e], value)

    @pl.when(pair == pl.num_programs(0) - 1)
    def _():
        out_ref[...] = out_all[: lats * block, :].astype(jnp.bfloat16).reshape(out_ref.shape)


def spectral_chunk(pieces, table, vertical, first, second, lower, chunk, shape, *ready):
    lats, levs, wire_rows, _ = shape
    columns, packed, all_lats = table.shape
    pairs = ROWS // 4
    rows = lats * levs * wire_rows
    plane = pieces[0].shape[0]
    block = (plane, rows // plane // len(pieces), LANES)
    return pl.pallas_call(
        functools.partial(spectral_kernel, len(pieces)),
        out_shape=jax.ShapeDtypeStruct(shape, jnp.bfloat16),
        grid_spec=pltpu.PrefetchScalarGridSpec(
            num_scalar_prefetch=1,
            grid=(pairs,),
            in_specs=[pl.BlockSpec(block, lambda p, _: (0, 0, 0))] * len(pieces)
            + [
                pl.BlockSpec((4, packed, all_lats), lambda p, _: (chunk * pairs + p, 0, 0)),
                pl.BlockSpec(vertical.shape, lambda p, _: (0, 0)),
                pl.BlockSpec(first.shape, lambda p, _: (0, 0)),
                pl.BlockSpec(second.shape, lambda p, _: (0, 0)),
            ]
            + [ANYWHERE] * len(ready),
            out_specs=pl.BlockSpec(shape, lambda p, _: (0, 0, 0, 0)),
            scratch_shapes=[
                pltpu.VMEM((rows + 4 * ROWS, LANES), jnp.float32),
                pltpu.VMEM((rows + 4 * ROWS, LANES), jnp.float32),
            ],
        ),
        compiler_params=pltpu.CompilerParams(vmem_limit_bytes=VMEM),
        cost_estimate=LONG,
        name="spectral_chunk",
    )(lower, *pieces, table, vertical, first, second, *ready)


def synthesis_kernel(pieces, parity_ref, *refs):
    field_refs, (table_ref, wind_ref) = refs[:pieces], refs[pieces : pieces + 2]
    out_ref, lines_ref = refs[-2:]
    half = LANES // 2
    whole = pl.ds(pl.multiple_of(half * parity_ref[0], half), LANES)
    rest = pl.ds(pl.multiple_of(LANES * (1 - parity_ref[0]), half), half)
    fields = jnp.concatenate([ref[...].astype(jnp.float32) for ref in field_refs], axis=0)
    for t in range(6):
        tile = fields[:, t * ROWS : (t + 1) * ROWS, :].reshape(-1, LANES)
        lines_ref[t * LANES : (t + 1) * LANES, :] = tile.astype(jnp.bfloat16).T

    sums = dot(lines_ref[...], table_ref[...], ((1,), (0,)))

    def put(t, j, rows, value):
        gain = wind_ref[t, 0, j, rows, :].astype(jnp.float32)
        out_ref[t, 0, j, rows, :] = (value * gain).astype(jnp.bfloat16)

    for j in range(2):
        first = j * 3 * LANES
        for t in range(2):
            put(t, j, whole, sums[first + t * LANES : first + (t + 1) * LANES])
            start = first + 2 * LANES + t * half
            put(t, j, rest, sums[start : start + half])


def synthesis_part(fields, table, wind, parity, start, count, before):
    _, _, _, lat_rows, points = wind.shape
    columns = table.shape[0]
    rows = 6 * ROWS

    def field_spec(array, first):
        return pl.BlockSpec((array.shape[0], rows, LANES), lambda s, _: (0, first + s, 0))

    grid_spec = pl.BlockSpec(
        (2, 1, 2, lat_rows, points), lambda s, _: (0, start + s, 0, 0, 0)
    )
    in_specs = [field_spec(*f) for f in fields]
    in_specs += [
        pl.BlockSpec((columns, points), lambda s, _: (0, 0)),
        grid_spec,
    ]
    operands = [f for f, _ in fields] + [table, wind]
    aliases = {}
    if before is not None:
        in_specs.append(ANYWHERE)
        aliases = {1 + len(operands): 0}
        operands.append(before)
    return pl.pallas_call(
        functools.partial(synthesis_kernel, len(fields)),
        out_shape=jax.ShapeDtypeStruct(wind.shape, jnp.bfloat16),
        grid_spec=pltpu.PrefetchScalarGridSpec(
            num_scalar_prefetch=1,
            grid=(count,),
            in_specs=in_specs,
            out_specs=grid_spec,
            scratch_shapes=[pltpu.VMEM((6 * LANES, columns), jnp.bfloat16)],
        ),
        input_output_aliases=aliases,
        compiler_params=pltpu.CompilerParams(vmem_limit_bytes=VMEM),
        cost_estimate=LONG,
        name="synthesis_part",
    )(parity, *operands)


def after_kernel(*refs):
    del refs


def after(x, *ready):
    return pl.pallas_call(
        after_kernel,
        out_shape=jax.ShapeDtypeStruct(x.shape, x.dtype),
        in_specs=[ANYWHERE] * (1 + len(ready)),
        out_specs=ANYWHERE,
        input_output_aliases={0: 0},
        cost_estimate=LONG,
        name="after",
    )(x, *ready)


def join_kernel(count, *refs):
    out_ref = refs[-1]
    rows = refs[0].shape[1]
    for k in range(count):
        out_ref[:, k * rows : (k + 1) * rows, :] = refs[k][...]


def join_slots(pieces, *ready):
    plane, rows, _ = pieces[-1].shape
    all_rows = len(pieces) * rows
    return pl.pallas_call(
        functools.partial(join_kernel, len(pieces)),
        out_shape=jax.ShapeDtypeStruct((plane, all_rows, LANES), jnp.bfloat16),
        grid=(2,),
        in_specs=[pl.BlockSpec((plane // 2, rows, LANES), lambda s: (s, 0, 0))] * len(pieces)
        + [ANYWHERE] * len(ready),
        out_specs=pl.BlockSpec((plane // 2, all_rows, LANES), lambda s: (s, 0, 0)),
        cost_estimate=LONG,
        name="join_slots",
    )(*pieces, *ready)


def part_kernel(layers, cuts, *refs):
    in_ref, out_refs = refs[0], refs[len(refs) - len(cuts) * (layers - 1) :]
    rows = in_ref.shape[1] // layers
    for i, out_ref in enumerate(out_refs):
        p, k = divmod(i, layers - 1)
        start = (k + 1) * rows + cuts[p][0]
        out_ref[...] = in_ref[:, start : start + cuts[p][1], :]


def part_slots(joined, layers, cuts, *ready):
    plane, rows, _ = joined.shape
    cuts = cuts or [(0, rows // layers)]
    sizes = [size for _, size in cuts for _ in range(layers - 1)]
    slots = pl.pallas_call(
        functools.partial(part_kernel, layers, cuts),
        out_shape=[jax.ShapeDtypeStruct((plane, n, LANES), jnp.bfloat16) for n in sizes],
        grid=(2,),
        in_specs=[pl.BlockSpec((plane // 2, rows, LANES), lambda s: (s, 0, 0))]
        + [ANYWHERE] * len(ready),
        out_specs=[pl.BlockSpec((plane // 2, n, LANES), lambda s: (s, 0, 0)) for n in sizes],
        cost_estimate=LONG,
        name="part_slots",
    )(joined, *ready)
    return [slots[p * (layers - 1) : (p + 1) * (layers - 1)] for p in range(len(cuts))]


def turn_along_z(slots, sign):
    lev_devices = lax.axis_size("lev")
    moved = []
    for k, slot in enumerate(slots, 1):
        pairs = [(b, (b + sign * CORES * k) % lev_devices) for b in range(lev_devices)]
        moved.append(lax.ppermute(slot, "lev", pairs))
    return moved


def exchange_in_plane(x, groups):
    return lax.all_to_all(
        x, ("lat", "lev"), split_axis=0, concat_axis=0, tiled=True, axis_index_groups=groups
    )


def turned(x, axis, start):
    size = x.shape[axis]
    return lax.dynamic_slice_in_dim(jnp.concatenate([x, x], axis=axis), start, size, axis)


def pipelined_body(adjoint_grid, wind, legendre, vertical, pair_table, degree_matrix):
    level_rows, lat_rows, points = adjoint_grid.shape
    lats = lax.axis_size("lat")
    levs = lax.axis_size("lev")
    layers = levs // CORES
    plane = lats * CORES
    slots, all_lats, packed = legendre.shape
    matrices, levels, _ = vertical.shape
    chunks = slots // ROWS
    pairs = ROWS // 4
    steps = level_rows // 4
    wire_rows = steps * 6 * ROWS

    lat, lev = lax.axis_index("lat"), lax.axis_index("lev")
    layer = lev // CORES
    parity = (lat % 2).astype(jnp.int32).reshape(1)
    groups = [
        [a * levs + z * CORES + c for a in range(lats) for c in range(CORES)] for z in range(layers)
    ]

    table_pairs = turned(pair_table.reshape(lats, layers, CORES, chunks, pairs), 1, layer)
    table_pairs = table_pairs.transpose(3, 1, 0, 2, 4)
    waves = jnp.stack([table_pairs, N - 1 - table_pairs], axis=-1)
    waves = jnp.broadcast_to(waves[..., None], waves.shape + (2,))
    waves = waves.reshape(chunks, layers, plane, ROWS)

    grid = adjoint_grid.reshape(2, steps, 2, lat_rows, points)
    wind = wind.reshape(2, steps, 2, lat_rows, points)
    table = legendre.transpose(0, 2, 1)

    slot_level = jnp.arange(levels, dtype=jnp.int32).reshape(layers, CORES, 2, level_rows // 2)
    slot_level = turned(jnp.flip(slot_level, 0), 0, layers - 1 - layer)
    slot_level = slot_level.transpose(2, 1, 0, 3).reshape(levels)
    order = (slot_level[:, None] == jnp.arange(levels)[None, :]).astype(jnp.bfloat16)
    operators = jnp.einsum("av,gvo->gao", order, vertical, preferred_element_type=jnp.float32)
    operators = jnp.einsum(
        "gao,bo->gab", operators.astype(jnp.bfloat16), order, preferred_element_type=jnp.float32
    )
    operators = operators.astype(jnp.bfloat16).reshape(matrices // 2, 2, levels, levels)
    operators = operators.transpose(0, 2, 1, 3).reshape(matrices // 2 * levels, 2 * levels)

    by_degree = jnp.concatenate([degree_matrix, jnp.broadcast_to(degree_matrix[-1:], (packed,))])
    second = jnp.concatenate([degree_matrix[:1], by_degree[: packed - 1]])
    first = jnp.broadcast_to(by_degree[:, None], (by_degree.shape[0], LANES))
    second = jnp.broadcast_to(second[:, None], (packed, LANES))
    first_pair = (lat * levs + lev) * (slots // 4)
    lower = lax.dynamic_slice(pair_table, (first_pair,), (slots // 4,)).reshape(chunks, pairs)

    joined_shape = (plane, layers * wire_rows, LANES)

    def across(x):
        return exchange_in_plane(x, groups)

    def along(first_slot, slots):
        return [first_slot] + turn_along_z(slots, 1)

    def home(first_slot, slots):
        return [first_slot] + turn_along_z(slots, -1)

    def solve(q, pieces, *ready):
        shape = (lats, levs, wire_rows, LANES)
        x = spectral_chunk(pieces, table, operators, first, second, lower[q], q, shape, *ready)
        return x.reshape(joined_shape)

    turned_waves = waves.transpose(0, 2, 1, 3)
    rows = jnp.stack([waves[0].reshape(-1), turned_waves[2].reshape(-1)]).reshape(-1, 1)
    sent = fourier_some(grid, rows, parity, [plane] * layers + [plane * layers])
    z0 = along(sent[0], sent[1:layers])
    x2 = sent[layers].reshape(joined_shape)
    rows = jnp.stack([turned_waves[1], turned_waves[3]]).reshape(-1, 1)
    sent = fourier_some(grid, rows, parity, [plane * layers] * 2, x2)
    x1, x3 = [x.reshape(joined_shape) for x in sent]
    p2 = across(x2)
    rows = jnp.stack([waves[0], waves[2], waves[3], waves[1]]).reshape(-1, 1)
    synthesis = synthesis_rows(rows, points, ROWS * layers * plane, x2)
    x3 = after(x3, p2, synthesis)
    p3 = across(x3)
    z1 = along(x1, part_slots(x1, layers, None, x3)[0])
    j0 = after(join_slots(z0, x3), p3)
    p0 = across(j0)
    u2 = part_slots(p2, layers, None, j0)[0]
    z2 = along(p2, u2)
    s0 = solve(0, [p0], u2[0])
    r0 = across(s0)
    j1 = join_slots(z1, s0)
    u3 = part_slots(p3, layers, None, j1)[0]
    z3 = along(p3, u3)
    j1 = after(j1, r0, u3[0])
    p1 = across(j1)
    b0 = part_slots(r0, layers, None, j1)[0]
    back0 = home(r0, b0)
    s2 = after(solve(2, z2, b0[0]), p1)
    r2 = across(s2)
    s3 = after(solve(3, z3, s2), r2)
    r3 = across(s3)
    b2 = part_slots(r2, layers, None, s3)[0]
    back2 = home(r2, b2)
    s1 = after(solve(1, [p1], b2[0]), r3)
    r1 = across(s1)
    b3 = part_slots(r3, layers, None, s1)[0]
    back3 = home(r3, b3)
    parts = [(0, steps // 2), (steps // 2, steps // 2)] if steps % 2 == 0 else [(0, steps)]
    cuts = [(6 * ROWS * first, 6 * ROWS * count) for first, count in parts]
    late = [home(r1, part) for part in part_slots(r1, layers, cuts, b3[0])]

    out = None
    for (first, count), part in zip(parts, late):
        here = [(f, first) for f in [*back0, *back2, *back3, part[0]]]
        here += [(f, 0) for f in part[1:]]
        out = synthesis_part(here, synthesis, wind, parity, first, count, out)
    return out.reshape(level_rows, lat_rows, points)


def body(adjoint_grid, wind, legendre, vertical, pair_table, degree_matrix):
    level_rows, lat_rows, points = adjoint_grid.shape
    lats, levs = lax.axis_size("lat"), lax.axis_size("lev")
    layers = levs // CORES
    fits = (
        levs % CORES == 0
        and lats % 2 == 0
        and lat_rows == LANES + LANES // 2
        and level_rows % 16 == 0
        and vertical.shape[0] % 2 == 0
        and vertical.shape[1] == LANES
        and points % LANES == 0
        and points // LANES <= LANES
        and legendre.shape[0] % ROWS == 0
        and legendre.shape[0] // ROWS == 4
        and legendre.shape[2] % 8 == 0
        and legendre.shape[2] > N
        and pair_table.shape[0] * 4 == legendre.shape[0] * lats * levs
    )
    plan = pipelined_body if fits else general_body
    return plan(adjoint_grid, wind, legendre, vertical, pair_table, degree_matrix)


def solution(mesh):
    placed = (
        P("lev", "lat", None),
        P("lev", "lat", None),
        P(("lat", "lev"), None, None),
        P(),
        P(),
        P(),
    )
    return jax.shard_map(
        body, mesh=mesh, in_specs=placed, out_specs=P("lev", "lat", None), check_vma=False
    )
```

```python
import functools
import math

import jax
import jax.numpy as jnp
from jax import lax
from jax.experimental import pallas as pl
from jax.experimental.pallas import tpu as pltpu
from jax.sharding import PartitionSpec as P

N = 512
CORES = 2
ROWS = 8
LANES = 128
VMEM = 48 * 2**20
LONG = pl.CostEstimate(flops=10**13, bytes_accessed=10**8, transcendentals=0)
SIN = (-1.0 / 39916800, 1.0 / 362880, -1.0 / 5040, 1.0 / 120, -1.0 / 6, 1.0)
ANYWHERE = pl.BlockSpec(memory_space=pl.ANY)


def fourier_basis(wavenumbers, points):
    longitude = jnp.arange(points, dtype=jnp.int32)
    phases = wavenumbers[:, :, None] * longitude[None, None, :] % points
    angles = phases.astype(jnp.float32) * (2.0 * jnp.pi / points)
    basis = jnp.stack([jnp.cos(angles), -jnp.sin(angles)], axis=2)
    return basis.reshape(-1, points)


def member_layout(lower_wave, row_total):
    packed_buffer = jnp.arange(row_total, dtype=jnp.int32)
    first_member = packed_buffer[None, :] < (N - lower_wave)[:, None]
    second_member = jnp.logical_not(first_member) & (packed_buffer[None, :] <= N)
    degree = jnp.where(
        first_member, lower_wave[:, None] + packed_buffer[None, :], packed_buffer[None, :] - 1
    )
    degree = jnp.clip(degree, 0, N - 1)
    return (first_member, second_member, degree)


def solve_columns(spectral_state, matrix_index, vertical):

    def add_matrix(operator_index, running):
        product = jnp.einsum(
            "xjm,mg->xjg",
            spectral_state,
            vertical[operator_index],
            preferred_element_type=jnp.float32,
        )
        return running + jnp.where((matrix_index == operator_index)[:, :, None], product, 0.0)

    zero_sums = jnp.zeros(spectral_state.shape, jnp.float32)
    return lax.fori_loop(0, vertical.shape[0], add_matrix, zero_sums).astype(jnp.bfloat16)


def general_body(adjoint_grid, wind, legendre, vertical, pair_table, degree_matrix):
    vertical_level_rows, lat_rows, points = adjoint_grid.shape
    lat_devices = lax.axis_size("lat")
    lev_devices = lax.axis_size("lev")
    slots = legendre.shape[0]
    all_lats = legendre.shape[1]
    packed_rows = legendre.shape[2]
    levels = vertical.shape[1]
    wavenumbers = jnp.stack([pair_table, N - 1 - pair_table], axis=1)
    basis = fourier_basis(wavenumbers, points)
    analysis_table = (basis * (1.0 / math.sqrt(points))).astype(jnp.bfloat16)
    synthesis_table = (basis * (1.0 / math.sqrt(N))).astype(jnp.bfloat16)
    fourier = jnp.einsum(
        "cx,vlx->cvl", analysis_table, adjoint_grid, preferred_element_type=jnp.float32
    )
    fourier = fourier.astype(jnp.bfloat16).reshape(
        lat_devices, lev_devices, slots, vertical_level_rows, lat_rows
    )
    moved = lax.all_to_all(
        lax.all_to_all(fourier, "lev", split_axis=1, concat_axis=3, tiled=True),
        "lat",
        split_axis=0,
        concat_axis=4,
        tiled=True,
    )
    field_stack = moved.reshape(slots, levels, all_lats)
    first_slot = (lax.axis_index("lat") * lev_devices + lax.axis_index("lev")) * slots
    column = first_slot + jnp.arange(slots, dtype=jnp.int32)
    lower_cols = jnp.take(pair_table, column // 4)
    member = column // 2 % 2
    first_member, second_member, degree = member_layout(lower_cols, packed_rows)
    own_rows = jnp.where((member == 0)[:, None], first_member, second_member).astype(jnp.float32)
    spectral_state = jnp.einsum(
        "peq,pae->pqa", legendre, field_stack, preferred_element_type=jnp.float32
    )
    spectral_state = (spectral_state * own_rows[:, :, None]).astype(jnp.bfloat16)
    matrix_index = jnp.take(degree_matrix, degree)
    solved_columns = solve_columns(spectral_state, matrix_index, vertical)
    gridpoint_coefficients = jnp.einsum(
        "ncb,nba->nac", legendre, solved_columns, preferred_element_type=jnp.float32
    )
    gridpoint_coefficients = gridpoint_coefficients.astype(jnp.bfloat16).reshape(
        1, 1, slots, levels, all_lats
    )
    returned = lax.all_to_all(
        lax.all_to_all(gridpoint_coefficients, "lat", split_axis=4, concat_axis=0, tiled=True),
        "lev",
        split_axis=3,
        concat_axis=1,
        tiled=True,
    )
    columns = returned.reshape(lat_devices * lev_devices * slots, vertical_level_rows, lat_rows)
    regridded = jnp.einsum(
        "cvl,cx->vlx", columns, synthesis_table, preferred_element_type=jnp.float32
    )
    return (regridded * wind.astype(jnp.float32)).astype(jnp.bfloat16)


def dot(a, b, dims):
    return lax.dot_general(a, b, (dims, ((), ())), preferred_element_type=jnp.float32)


def cos_turn(steps, points):
    rest = steps - points * jnp.floor(steps * (1.0 / points) + 0.5)
    angle = (points // 4 - jnp.abs(rest)) * (2.0 * math.pi / points)
    square = angle * angle
    total = jnp.full_like(square, SIN[0])
    for c in SIN[1:]:
        total = total * square + c
    return total * angle


def make_table(wave, points, scale):
    rows = wave.shape[0]
    lane = lax.broadcasted_iota(jnp.int32, (rows, LANES), 1).astype(jnp.float32)
    part = lax.broadcasted_iota(jnp.int32, (rows, LANES), 0) % 2
    shift = (part * (points // 4)).astype(jnp.float32)
    waves = jnp.broadcast_to(wave, (rows, LANES)).astype(jnp.float32)
    twice = 2.0 * cos_turn(waves * LANES, points)
    tiles = [cos_turn(waves * (lane + i * LANES) + shift, points) * scale for i in range(2)]
    while len(tiles) < points // LANES:
        tiles.append(twice * tiles[-1] - tiles[-2])
    return jnp.concatenate(tiles, axis=1).astype(jnp.bfloat16)


def fourier_kernel(waits, parity_ref, wave_ref, grid_ref, *refs):
    out_refs, table_ref = refs[waits:-1], refs[-1]
    points = grid_ref.shape[-1]
    rows = sum(ref.shape[0] for ref in out_refs) * ROWS

    @pl.when(pl.program_id(0) == 0)
    def _():
        block = ROWS * 32

        def fill(i, _):
            at = pl.ds(pl.multiple_of(i * block, block), block)
            table_ref[at, :] = make_table(wave_ref[at, :], points, 1.0 / math.sqrt(points))
            return 0

        lax.fori_loop(0, rows // block, fill, 0)

    half = LANES // 2
    whole = pl.ds(pl.multiple_of(half * parity_ref[0], half), LANES)
    rest = pl.ds(pl.multiple_of(LANES * (1 - parity_ref[0]), half), half)
    lines = []
    for j in range(2):
        lines += [grid_ref[t, 0, j, whole, :] for t in range(2)]
        lines += [grid_ref[t, 0, j, rest, :] for t in range(2)]
    lines = jnp.concatenate(lines, axis=0)
    sums = dot(table_ref[...], lines, ((1,), (1,)))
    sums = sums.reshape(-1, ROWS, sums.shape[1])
    start = 0
    for ref in out_refs:
        part = sums[start : start + ref.shape[0]]
        tiles = [part[:, :, t * LANES : (t + 1) * LANES] for t in range(6)]
        ref[...] = jnp.concatenate(tiles, axis=1).astype(jnp.bfloat16)
        start += ref.shape[0]


def fourier_some(grid, wave, parity, slots, *ready):
    _, steps, _, lat_rows, points = grid.shape
    columns = wave.shape[0]
    rows = 6 * ROWS
    return pl.pallas_call(
        functools.partial(fourier_kernel, len(ready)),
        out_shape=[jax.ShapeDtypeStruct((n, steps * rows, LANES), jnp.bfloat16) for n in slots],
        grid_spec=pltpu.PrefetchScalarGridSpec(
            num_scalar_prefetch=1,
            grid=(steps,),
            in_specs=[
                pl.BlockSpec((columns, 1), lambda s, _: (0, 0)),
                pl.BlockSpec((2, 1, 2, lat_rows, points), lambda s, _: (0, s, 0, 0, 0)),
            ]
            + [ANYWHERE] * len(ready),
            out_specs=[pl.BlockSpec((n, rows, LANES), lambda s, _: (0, s, 0)) for n in slots],
            scratch_shapes=[pltpu.VMEM((columns, points), jnp.bfloat16)],
        ),
        compiler_params=pltpu.CompilerParams(vmem_limit_bytes=VMEM),
        cost_estimate=LONG,
        name="fourier_some",
    )(parity, wave, grid, *ready)


def table_kernel(wave_ref, *refs):
    out_ref = refs[-1]
    out_ref[...] = make_table(wave_ref[...], out_ref.shape[1], 1.0 / math.sqrt(N))


def synthesis_rows(wave, points, block, *ready):
    columns = wave.shape[0]
    return pl.pallas_call(
        table_kernel,
        out_shape=jax.ShapeDtypeStruct((columns, points), jnp.bfloat16),
        grid=(columns // block,),
        in_specs=[pl.BlockSpec((block, 1), lambda s: (s, 0))] + [ANYWHERE] * len(ready),
        out_specs=pl.BlockSpec((block, points), lambda s: (s, 0)),
        compiler_params=pltpu.CompilerParams(vmem_limit_bytes=VMEM),
        cost_estimate=LONG,
        name="synthesis_rows",
    )(wave, *ready)


def spectral_kernel(pieces, lower_ref, *refs):
    field_refs = refs[:pieces]
    table_ref, vertical_ref, first_ref, second_ref = refs[pieces : pieces + 4]
    out_ref, field_all, out_all = refs[-3:]
    pair = pl.program_id(0)
    lats, levs, wire_rows, _ = out_ref.shape
    stride = 3 * ROWS
    count = levs * wire_rows // stride
    block = levs * wire_rows
    half = LANES // 2
    packed = table_ref.shape[1]
    couples = vertical_ref.shape[0] // LANES
    middle_row = N // 2

    @pl.when(pair == 0)
    def _():
        plane, rows, _ = field_refs[0].shape
        for i in range(plane):
            for k, ref in enumerate(field_refs):
                start = (i * pieces + k) * rows
                field_all[start : start + rows, :] = ref[i].astype(jnp.float32)

    left = lax.broadcasted_iota(jnp.int32, (count, LANES), 1) < half
    lower = lower_ref[pair]
    row = lax.broadcasted_iota(jnp.int32, (packed, LANES), 0)
    own = row < N - lower
    operator = jnp.where(own, first_ref[pl.ds(lower, packed), :], second_ref[...])
    couple = operator // 2
    odd = operator % 2 == 1
    own = own[middle_row:]
    valid = row[middle_row:] <= N

    def at(lat, t, column):
        return pl.ds(lat * block + t * ROWS + column, count, stride=stride)

    def swap(x):
        return pltpu.roll(x, half, 1)

    def read_field(column):
        tiles = []
        for lat in range(0, lats, 2):
            low = field_all[at(lat, 2, column), :]
            high = field_all[at(lat + 1, 2, column), :]
            middle = [jnp.where(left, low, swap(high)), jnp.where(left, swap(low), high)]
            tiles.append([field_all[at(lat, t, column), :] for t in range(2)])
            tiles.append(middle)
            tiles.append([field_all[at(lat + 1, t, column), :] for t in range(2)])
        levels = [jnp.concatenate([tile[t] for tile in tiles], axis=1) for t in range(2)]
        return jnp.concatenate(levels, axis=0).astype(jnp.bfloat16)

    def write_field(column, value):
        for lat in range(0, lats, 2):
            first = lat // 2 * 3 * LANES
            tile = [value[:, first + i * LANES : first + (i + 1) * LANES] for i in range(3)]
            parts = [[x[:count], x[count:]] for x in tile]
            for t in range(2):
                out_all[at(lat, t, column), :] = parts[0][t]
                out_all[at(lat + 1, t, column), :] = parts[2][t]
            out_all[at(lat, 2, column), :] = jnp.where(left, parts[1][0], swap(parts[1][1]))
            out_all[at(lat + 1, 2, column), :] = jnp.where(left, swap(parts[1][0]), parts[1][1])

    for r in range(2):
        columns = [4 * pair + 2 * e + r for e in range(2)]
        tables = [table_ref.at[r, :N], table_ref.at[2 + r, middle_row:]]
        state = [dot(tables[e][...], read_field(columns[e]), ((1,), (1,))) for e in range(2)]
        upper = jnp.concatenate(
            [state[0][middle_row:], jnp.zeros((packed - N, LANES), jnp.float32)], axis=0
        )
        upper = jnp.where(own, upper, jnp.where(valid, state[1], 0.0))
        spectral = jnp.concatenate([state[0][:middle_row], upper], axis=0)
        spectral = spectral.astype(jnp.bfloat16).astype(jnp.float32)
        spread = [jnp.where(couple == g, spectral, 0.0).astype(jnp.bfloat16) for g in range(couples)]
        solved = dot(jnp.concatenate(spread, axis=1), vertical_ref[...], ((1,), (0,)))
        solved = jnp.where(odd, solved[:, LANES:], solved[:, :LANES])
        upper = solved[middle_row:]
        mine = [
            jnp.concatenate(
                [solved[:middle_row], jnp.where(own, upper, 0.0)[: N - middle_row]], axis=0
            ),
            jnp.where(own, 0.0, upper),
        ]
        for e in range(2):
            value = dot(mine[e].astype(jnp.bfloat16), tables[e][...], ((0,), (0,)))
            write_field(columns[e], value)

    @pl.when(pair == pl.num_programs(0) - 1)
    def _():
        out_ref[...] = out_all[: lats * block, :].astype(jnp.bfloat16).reshape(out_ref.shape)


def spectral_chunk(pieces, table, vertical, first, second, lower, chunk, shape, *ready):
    lats, levs, wire_rows, _ = shape
    columns, packed, all_lats = table.shape
    pairs = ROWS // 4
    rows = lats * levs * wire_rows
    plane = pieces[0].shape[0]
    block = (plane, rows // plane // len(pieces), LANES)
    return pl.pallas_call(
        functools.partial(spectral_kernel, len(pieces)),
        out_shape=jax.ShapeDtypeStruct(shape, jnp.bfloat16),
        grid_spec=pltpu.PrefetchScalarGridSpec(
            num_scalar_prefetch=1,
            grid=(pairs,),
            in_specs=[pl.BlockSpec(block, lambda p, _: (0, 0, 0))] * len(pieces)
            + [
                pl.BlockSpec((4, packed, all_lats), lambda p, _: (chunk * pairs + p, 0, 0)),
                pl.BlockSpec(vertical.shape, lambda p, _: (0, 0)),
                pl.BlockSpec(first.shape, lambda p, _: (0, 0)),
                pl.BlockSpec(second.shape, lambda p, _: (0, 0)),
            ]
            + [ANYWHERE] * len(ready),
            out_specs=pl.BlockSpec(shape, lambda p, _: (0, 0, 0, 0)),
            scratch_shapes=[
                pltpu.VMEM((rows + 4 * ROWS, LANES), jnp.float32),
                pltpu.VMEM((rows + 4 * ROWS, LANES), jnp.float32),
            ],
        ),
        compiler_params=pltpu.CompilerParams(vmem_limit_bytes=VMEM),
        cost_estimate=LONG,
        name="spectral_chunk",
    )(lower, *pieces, table, vertical, first, second, *ready)


def synthesis_kernel(pieces, parity_ref, *refs):
    field_refs, (table_ref, wind_ref) = refs[:pieces], refs[pieces : pieces + 2]
    out_ref, lines_ref = refs[-2:]
    half = LANES // 2
    whole = pl.ds(pl.multiple_of(half * parity_ref[0], half), LANES)
    rest = pl.ds(pl.multiple_of(LANES * (1 - parity_ref[0]), half), half)
    fields = jnp.concatenate([ref[...].astype(jnp.float32) for ref in field_refs], axis=0)
    for t in range(6):
        tile = fields[:, t * ROWS : (t + 1) * ROWS, :].reshape(-1, LANES)
        lines_ref[t * LANES : (t + 1) * LANES, :] = tile.astype(jnp.bfloat16).T

    sums = dot(lines_ref[...], table_ref[...], ((1,), (0,)))

    def put(t, j, rows, value):
        gain = wind_ref[t, 0, j, rows, :].astype(jnp.float32)
        out_ref[t, 0, j, rows, :] = (value * gain).astype(jnp.bfloat16)

    for j in range(2):
        first = j * 3 * LANES
        for t in range(2):
            put(t, j, whole, sums[first + t * LANES : first + (t + 1) * LANES])
            start = first + 2 * LANES + t * half
            put(t, j, rest, sums[start : start + half])


def synthesis_part(fields, table, wind, parity, start, count, before):
    _, _, _, lat_rows, points = wind.shape
    columns = table.shape[0]
    rows = 6 * ROWS

    def field_spec(array, first):
        return pl.BlockSpec((array.shape[0], rows, LANES), lambda s, _: (0, first + s, 0))

    grid_spec = pl.BlockSpec(
        (2, 1, 2, lat_rows, points), lambda s, _: (0, start + s, 0, 0, 0)
    )
    in_specs = [field_spec(*f) for f in fields]
    in_specs += [
        pl.BlockSpec((columns, points), lambda s, _: (0, 0)),
        grid_spec,
    ]
    operands = [f for f, _ in fields] + [table, wind]
    aliases = {}
    if before is not None:
        in_specs.append(ANYWHERE)
        aliases = {1 + len(operands): 0}
        operands.append(before)
    return pl.pallas_call(
        functools.partial(synthesis_kernel, len(fields)),
        out_shape=jax.ShapeDtypeStruct(wind.shape, jnp.bfloat16),
        grid_spec=pltpu.PrefetchScalarGridSpec(
            num_scalar_prefetch=1,
            grid=(count,),
            in_specs=in_specs,
            out_specs=grid_spec,
            scratch_shapes=[pltpu.VMEM((6 * LANES, columns), jnp.bfloat16)],
        ),
        input_output_aliases=aliases,
        compiler_params=pltpu.CompilerParams(vmem_limit_bytes=VMEM),
        cost_estimate=LONG,
        name="synthesis_part",
    )(parity, *operands)


def after_kernel(*refs):
    del refs


def after(x, *ready):
    return pl.pallas_call(
        after_kernel,
        out_shape=jax.ShapeDtypeStruct(x.shape, x.dtype),
        in_specs=[ANYWHERE] * (1 + len(ready)),
        out_specs=ANYWHERE,
        input_output_aliases={0: 0},
        cost_estimate=LONG,
        name="after",
    )(x, *ready)


def join_kernel(count, *refs):
    out_ref = refs[-1]
    rows = refs[0].shape[1]
    for k in range(count):
        out_ref[:, k * rows : (k + 1) * rows, :] = refs[k][...]


def join_slots(pieces, *ready):
    plane, rows, _ = pieces[-1].shape
    all_rows = len(pieces) * rows
    return pl.pallas_call(
        functools.partial(join_kernel, len(pieces)),
        out_shape=jax.ShapeDtypeStruct((plane, all_rows, LANES), jnp.bfloat16),
        grid=(2,),
        in_specs=[pl.BlockSpec((plane // 2, rows, LANES), lambda s: (s, 0, 0))] * len(pieces)
        + [ANYWHERE] * len(ready),
        out_specs=pl.BlockSpec((plane // 2, all_rows, LANES), lambda s: (s, 0, 0)),
        cost_estimate=LONG,
        name="join_slots",
    )(*pieces, *ready)


def part_kernel(layers, cuts, *refs):
    in_ref, out_refs = refs[0], refs[len(refs) - len(cuts) * (layers - 1) :]
    rows = in_ref.shape[1] // layers
    for i, out_ref in enumerate(out_refs):
        p, k = divmod(i, layers - 1)
        start = (k + 1) * rows + cuts[p][0]
        out_ref[...] = in_ref[:, start : start + cuts[p][1], :]


def part_slots(joined, layers, cuts, *ready):
    plane, rows, _ = joined.shape
    cuts = cuts or [(0, rows // layers)]
    sizes = [size for _, size in cuts for _ in range(layers - 1)]
    slots = pl.pallas_call(
        functools.partial(part_kernel, layers, cuts),
        out_shape=[jax.ShapeDtypeStruct((plane, n, LANES), jnp.bfloat16) for n in sizes],
        grid=(2,),
        in_specs=[pl.BlockSpec((plane // 2, rows, LANES), lambda s: (s, 0, 0))]
        + [ANYWHERE] * len(ready),
        out_specs=[pl.BlockSpec((plane // 2, n, LANES), lambda s: (s, 0, 0)) for n in sizes],
        cost_estimate=LONG,
        name="part_slots",
    )(joined, *ready)
    return [slots[p * (layers - 1) : (p + 1) * (layers - 1)] for p in range(len(cuts))]


def turn_along_z(slots, sign):
    lev_devices = lax.axis_size("lev")
    moved = []
    for k, slot in enumerate(slots, 1):
        pairs = [(b, (b + sign * CORES * k) % lev_devices) for b in range(lev_devices)]
        moved.append(lax.ppermute(slot, "lev", pairs))
    return moved


def exchange_in_plane(x, groups):
    return lax.all_to_all(
        x, ("lat", "lev"), split_axis=0, concat_axis=0, tiled=True, axis_index_groups=groups
    )


def turned(x, axis, start):
    size = x.shape[axis]
    return lax.dynamic_slice_in_dim(jnp.concatenate([x, x], axis=axis), start, size, axis)


def pipelined_body(adjoint_grid, wind, legendre, vertical, pair_table, degree_matrix):
    level_rows, lat_rows, points = adjoint_grid.shape
    lats = lax.axis_size("lat")
    levs = lax.axis_size("lev")
    layers = levs // CORES
    plane = lats * CORES
    slots, all_lats, packed = legendre.shape
    matrices, levels, _ = vertical.shape
    chunks = slots // ROWS
    pairs = ROWS // 4
    steps = level_rows // 4
    wire_rows = steps * 6 * ROWS

    lat, lev = lax.axis_index("lat"), lax.axis_index("lev")
    layer = lev // CORES
    parity = (lat % 2).astype(jnp.int32).reshape(1)
    groups = [
        [a * levs + z * CORES + c for a in range(lats) for c in range(CORES)] for z in range(layers)
    ]

    table_pairs = turned(pair_table.reshape(lats, layers, CORES, chunks, pairs), 1, layer)
    table_pairs = table_pairs.transpose(3, 1, 0, 2, 4)
    waves = jnp.stack([table_pairs, N - 1 - table_pairs], axis=-1)
    waves = jnp.broadcast_to(waves[..., None], waves.shape + (2,))
    waves = waves.reshape(chunks, layers, plane, ROWS)

    grid = adjoint_grid.reshape(2, steps, 2, lat_rows, points)
    wind = wind.reshape(2, steps, 2, lat_rows, points)
    table = legendre.transpose(0, 2, 1)

    slot_level = jnp.arange(levels, dtype=jnp.int32).reshape(layers, CORES, 2, level_rows // 2)
    slot_level = turned(jnp.flip(slot_level, 0), 0, layers - 1 - layer)
    slot_level = slot_level.transpose(2, 1, 0, 3).reshape(levels)
    order = (slot_level[:, None] == jnp.arange(levels)[None, :]).astype(jnp.bfloat16)
    operators = jnp.einsum("av,gvo->gao", order, vertical, preferred_element_type=jnp.float32)
    operators = jnp.einsum(
        "gao,bo->gab", operators.astype(jnp.bfloat16), order, preferred_element_type=jnp.float32
    )
    operators = operators.astype(jnp.bfloat16).reshape(matrices // 2, 2, levels, levels)
    operators = operators.transpose(0, 2, 1, 3).reshape(matrices // 2 * levels, 2 * levels)

    by_degree = jnp.concatenate([degree_matrix, jnp.broadcast_to(degree_matrix[-1:], (packed,))])
    second = jnp.concatenate([degree_matrix[:1], by_degree[: packed - 1]])
    first = jnp.broadcast_to(by_degree[:, None], (by_degree.shape[0], LANES))
    second = jnp.broadcast_to(second[:, None], (packed, LANES))
    first_pair = (lat * levs + lev) * (slots // 4)
    lower = lax.dynamic_slice(pair_table, (first_pair,), (slots // 4,)).reshape(chunks, pairs)

    joined_shape = (plane, layers * wire_rows, LANES)

    def across(x):
        return exchange_in_plane(x, groups)

    def along(first_slot, slots):
        return [first_slot] + turn_along_z(slots, 1)

    def home(first_slot, slots):
        return [first_slot] + turn_along_z(slots, -1)

    def solve(q, pieces, *ready):
        shape = (lats, levs, wire_rows, LANES)
        x = spectral_chunk(pieces, table, operators, first, second, lower[q], q, shape, *ready)
        return x.reshape(joined_shape)

    turned_waves = waves.transpose(0, 2, 1, 3)
    sent = fourier_some(grid, waves[0].reshape(-1, 1), parity, [plane] * layers)
    z0 = along(sent[0], sent[1:layers])
    rows = turned_waves[1:].reshape(-1, 1)
    sent = fourier_some(grid, rows, parity, [plane * layers] * 3, sent[0])
    x1, x2, x3 = [x.reshape(joined_shape) for x in sent]
    p2 = across(x2)
    rows = jnp.stack([waves[0], waves[2], waves[3], waves[1]]).reshape(-1, 1)
    synthesis = synthesis_rows(rows, points, ROWS * layers * plane, x2)
    u1 = part_slots(x1, layers, None, synthesis, *z0[1:])[0]
    z1 = along(x1, u1)
    j0 = after(join_slots(z0, u1[0]), p2)
    p0 = across(j0)
    u2 = part_slots(p2, layers, None, j0)[0]
    z2 = along(p2, u2)
    x3 = after(x3, p0, u2[0])
    p3 = across(x3)
    s0 = solve(0, [p0], x3)
    j1 = join_slots(z1, s0)
    s0 = after(s0, p3, j1)
    r0 = across(s0)
    u3 = part_slots(p3, layers, None, s0)[0]
    z3 = along(p3, u3)
    j1 = after(j1, r0, u3[0])
    p1 = across(j1)
    b0 = part_slots(r0, layers, None, j1)[0]
    back0 = home(r0, b0)
    s2 = after(solve(2, z2, b0[0]), p1)
    r2 = across(s2)
    s3 = after(solve(3, z3, s2), r2)
    r3 = across(s3)
    b2 = part_slots(r2, layers, None, s3)[0]
    back2 = home(r2, b2)
    s1 = after(solve(1, [p1], b2[0]), r3)
    r1 = across(s1)
    b3 = part_slots(r3, layers, None, s1)[0]
    back3 = home(r3, b3)
    parts = [(0, steps // 2), (steps // 2, steps // 2)] if steps % 2 == 0 else [(0, steps)]
    cuts = [(6 * ROWS * first, 6 * ROWS * count) for first, count in parts]
    late = [home(r1, part) for part in part_slots(r1, layers, cuts, b3[0])]

    out = None
    for (first, count), part in zip(parts, late):
        here = [(f, first) for f in [*back0, *back2, *back3, part[0]]]
        here += [(f, 0) for f in part[1:]]
        out = synthesis_part(here, synthesis, wind, parity, first, count, out)
    return out.reshape(level_rows, lat_rows, points)


def body(adjoint_grid, wind, legendre, vertical, pair_table, degree_matrix):
    level_rows, lat_rows, points = adjoint_grid.shape
    lats, levs = lax.axis_size("lat"), lax.axis_size("lev")
    layers = levs // CORES
    fits = (
        levs % CORES == 0
        and lats % 2 == 0
        and lat_rows == LANES + LANES // 2
        and level_rows % 16 == 0
        and vertical.shape[0] % 2 == 0
        and vertical.shape[1] == LANES
        and points % LANES == 0
        and points // LANES <= LANES
        and legendre.shape[0] % ROWS == 0
        and legendre.shape[0] // ROWS == 4
        and legendre.shape[2] % 8 == 0
        and legendre.shape[2] > N
        and pair_table.shape[0] * 4 == legendre.shape[0] * lats * levs
    )
    plan = pipelined_body if fits else general_body
    return plan(adjoint_grid, wind, legendre, vertical, pair_table, degree_matrix)


def solution(mesh):
    placed = (
        P("lev", "lat", None),
        P("lev", "lat", None),
        P(("lat", "lev"), None, None),
        P(),
        P(),
        P(),
    )
    return jax.shard_map(
        body, mesh=mesh, in_specs=placed, out_specs=P("lev", "lat", None), check_vma=False
    )
```

```python
import functools
import math

import jax
import jax.numpy as jnp
from jax import lax
from jax.experimental import pallas as pl
from jax.experimental.pallas import tpu as pltpu
from jax.sharding import PartitionSpec as P

N = 512
CORES = 2
ROWS = 8
LANES = 128
VMEM = 48 * 2**20
LONG = pl.CostEstimate(flops=10**13, bytes_accessed=10**8, transcendentals=0)
SIN = (-1.0 / 39916800, 1.0 / 362880, -1.0 / 5040, 1.0 / 120, -1.0 / 6, 1.0)
ANYWHERE = pl.BlockSpec(memory_space=pl.ANY)


def fourier_basis(wavenumbers, points):
    longitude = jnp.arange(points, dtype=jnp.int32)
    phases = wavenumbers[:, :, None] * longitude[None, None, :] % points
    angles = phases.astype(jnp.float32) * (2.0 * jnp.pi / points)
    basis = jnp.stack([jnp.cos(angles), -jnp.sin(angles)], axis=2)
    return basis.reshape(-1, points)


def member_layout(lower_wave, row_total):
    packed_buffer = jnp.arange(row_total, dtype=jnp.int32)
    first_member = packed_buffer[None, :] < (N - lower_wave)[:, None]
    second_member = jnp.logical_not(first_member) & (packed_buffer[None, :] <= N)
    degree = jnp.where(
        first_member, lower_wave[:, None] + packed_buffer[None, :], packed_buffer[None, :] - 1
    )
    degree = jnp.clip(degree, 0, N - 1)
    return (first_member, second_member, degree)


def solve_columns(spectral_state, matrix_index, vertical):

    def add_matrix(operator_index, running):
        product = jnp.einsum(
            "xjm,mg->xjg",
            spectral_state,
            vertical[operator_index],
            preferred_element_type=jnp.float32,
        )
        return running + jnp.where((matrix_index == operator_index)[:, :, None], product, 0.0)

    zero_sums = jnp.zeros(spectral_state.shape, jnp.float32)
    return lax.fori_loop(0, vertical.shape[0], add_matrix, zero_sums).astype(jnp.bfloat16)


def general_body(adjoint_grid, wind, legendre, vertical, pair_table, degree_matrix):
    vertical_level_rows, lat_rows, points = adjoint_grid.shape
    lat_devices = lax.axis_size("lat")
    lev_devices = lax.axis_size("lev")
    slots = legendre.shape[0]
    all_lats = legendre.shape[1]
    packed_rows = legendre.shape[2]
    levels = vertical.shape[1]
    wavenumbers = jnp.stack([pair_table, N - 1 - pair_table], axis=1)
    basis = fourier_basis(wavenumbers, points)
    analysis_table = (basis * (1.0 / math.sqrt(points))).astype(jnp.bfloat16)
    synthesis_table = (basis * (1.0 / math.sqrt(N))).astype(jnp.bfloat16)
    fourier = jnp.einsum(
        "cx,vlx->cvl", analysis_table, adjoint_grid, preferred_element_type=jnp.float32
    )
    fourier = fourier.astype(jnp.bfloat16).reshape(
        lat_devices, lev_devices, slots, vertical_level_rows, lat_rows
    )
    moved = lax.all_to_all(
        lax.all_to_all(fourier, "lev", split_axis=1, concat_axis=3, tiled=True),
        "lat",
        split_axis=0,
        concat_axis=4,
        tiled=True,
    )
    field_stack = moved.reshape(slots, levels, all_lats)
    first_slot = (lax.axis_index("lat") * lev_devices + lax.axis_index("lev")) * slots
    column = first_slot + jnp.arange(slots, dtype=jnp.int32)
    lower_cols = jnp.take(pair_table, column // 4)
    member = column // 2 % 2
    first_member, second_member, degree = member_layout(lower_cols, packed_rows)
    own_rows = jnp.where((member == 0)[:, None], first_member, second_member).astype(jnp.float32)
    spectral_state = jnp.einsum(
        "peq,pae->pqa", legendre, field_stack, preferred_element_type=jnp.float32
    )
    spectral_state = (spectral_state * own_rows[:, :, None]).astype(jnp.bfloat16)
    matrix_index = jnp.take(degree_matrix, degree)
    solved_columns = solve_columns(spectral_state, matrix_index, vertical)
    gridpoint_coefficients = jnp.einsum(
        "ncb,nba->nac", legendre, solved_columns, preferred_element_type=jnp.float32
    )
    gridpoint_coefficients = gridpoint_coefficients.astype(jnp.bfloat16).reshape(
        1, 1, slots, levels, all_lats
    )
    returned = lax.all_to_all(
        lax.all_to_all(gridpoint_coefficients, "lat", split_axis=4, concat_axis=0, tiled=True),
        "lev",
        split_axis=3,
        concat_axis=1,
        tiled=True,
    )
    columns = returned.reshape(lat_devices * lev_devices * slots, vertical_level_rows, lat_rows)
    regridded = jnp.einsum(
        "cvl,cx->vlx", columns, synthesis_table, preferred_element_type=jnp.float32
    )
    return (regridded * wind.astype(jnp.float32)).astype(jnp.bfloat16)


def dot(a, b, dims):
    return lax.dot_general(a, b, (dims, ((), ())), preferred_element_type=jnp.float32)


def cos_turn(steps, points):
    rest = steps - points * jnp.floor(steps * (1.0 / points) + 0.5)
    angle = (points // 4 - jnp.abs(rest)) * (2.0 * math.pi / points)
    square = angle * angle
    total = jnp.full_like(square, SIN[0])
    for c in SIN[1:]:
        total = total * square + c
    return total * angle


def make_table(wave, points, scale):
    rows = wave.shape[0]
    lane = lax.broadcasted_iota(jnp.int32, (rows, LANES), 1).astype(jnp.float32)
    part = lax.broadcasted_iota(jnp.int32, (rows, LANES), 0) % 2
    shift = (part * (points // 4)).astype(jnp.float32)
    waves = jnp.broadcast_to(wave, (rows, LANES)).astype(jnp.float32)
    twice = 2.0 * cos_turn(waves * LANES, points)
    tiles = [cos_turn(waves * (lane + i * LANES) + shift, points) * scale for i in range(2)]
    while len(tiles) < points // LANES:
        tiles.append(twice * tiles[-1] - tiles[-2])
    return jnp.concatenate(tiles, axis=1).astype(jnp.bfloat16)


def fourier_kernel(waits, parity_ref, wave_ref, grid_ref, *refs):
    out_refs, table_ref = refs[waits:-1], refs[-1]
    points = grid_ref.shape[-1]
    rows = sum(ref.shape[0] for ref in out_refs) * ROWS

    @pl.when(pl.program_id(0) == 0)
    def _():
        block = ROWS * 32

        def fill(i, _):
            at = pl.ds(pl.multiple_of(i * block, block), block)
            table_ref[at, :] = make_table(wave_ref[at, :], points, 1.0 / math.sqrt(points))
            return 0

        lax.fori_loop(0, rows // block, fill, 0)

    half = LANES // 2
    whole = pl.ds(pl.multiple_of(half * parity_ref[0], half), LANES)
    rest = pl.ds(pl.multiple_of(LANES * (1 - parity_ref[0]), half), half)
    lines = []
    for j in range(2):
        lines += [grid_ref[t, 0, j, whole, :] for t in range(2)]
        lines += [grid_ref[t, 0, j, rest, :] for t in range(2)]
    lines = jnp.concatenate(lines, axis=0)
    sums = dot(table_ref[...], lines, ((1,), (1,)))
    sums = sums.reshape(-1, ROWS, sums.shape[1])
    start = 0
    for ref in out_refs:
        part = sums[start : start + ref.shape[0]]
        tiles = [part[:, :, t * LANES : (t + 1) * LANES] for t in range(6)]
        ref[...] = jnp.concatenate(tiles, axis=1).astype(jnp.bfloat16)
        start += ref.shape[0]


def fourier_some(grid, wave, parity, slots, *ready):
    _, steps, _, lat_rows, points = grid.shape
    columns = wave.shape[0]
    rows = 6 * ROWS
    return pl.pallas_call(
        functools.partial(fourier_kernel, len(ready)),
        out_shape=[jax.ShapeDtypeStruct((n, steps * rows, LANES), jnp.bfloat16) for n in slots],
        grid_spec=pltpu.PrefetchScalarGridSpec(
            num_scalar_prefetch=1,
            grid=(steps,),
            in_specs=[
                pl.BlockSpec((columns, 1), lambda s, _: (0, 0)),
                pl.BlockSpec((2, 1, 2, lat_rows, points), lambda s, _: (0, s, 0, 0, 0)),
            ]
            + [ANYWHERE] * len(ready),
            out_specs=[pl.BlockSpec((n, rows, LANES), lambda s, _: (0, s, 0)) for n in slots],
            scratch_shapes=[pltpu.VMEM((columns, points), jnp.bfloat16)],
        ),
        compiler_params=pltpu.CompilerParams(vmem_limit_bytes=VMEM),
        cost_estimate=LONG,
        name="fourier_some",
    )(parity, wave, grid, *ready)


def table_kernel(wave_ref, *refs):
    out_ref = refs[-1]
    out_ref[...] = make_table(wave_ref[...], out_ref.shape[1], 1.0 / math.sqrt(N))


def synthesis_rows(wave, points, block, *ready):
    columns = wave.shape[0]
    return pl.pallas_call(
        table_kernel,
        out_shape=jax.ShapeDtypeStruct((columns, points), jnp.bfloat16),
        grid=(columns // block,),
        in_specs=[pl.BlockSpec((block, 1), lambda s: (s, 0))] + [ANYWHERE] * len(ready),
        out_specs=pl.BlockSpec((block, points), lambda s: (s, 0)),
        compiler_params=pltpu.CompilerParams(vmem_limit_bytes=VMEM),
        cost_estimate=LONG,
        name="synthesis_rows",
    )(wave, *ready)


def spectral_kernel(pieces, lower_ref, *refs):
    field_refs = refs[:pieces]
    table_ref, vertical_ref, first_ref, second_ref = refs[pieces : pieces + 4]
    out_ref, field_all, out_all = refs[-3:]
    pair = pl.program_id(0)
    lats, levs, wire_rows, _ = out_ref.shape
    stride = 3 * ROWS
    count = levs * wire_rows // stride
    block = levs * wire_rows
    half = LANES // 2
    packed = table_ref.shape[1]
    couples = vertical_ref.shape[0] // LANES
    middle_row = N // 2

    @pl.when(pair == 0)
    def _():
        plane, rows, _ = field_refs[0].shape
        for i in range(plane):
            for k, ref in enumerate(field_refs):
                start = (i * pieces + k) * rows
                field_all[start : start + rows, :] = ref[i].astype(jnp.float32)

    left = lax.broadcasted_iota(jnp.int32, (count, LANES), 1) < half
    lower = lower_ref[pair]
    row = lax.broadcasted_iota(jnp.int32, (packed, LANES), 0)
    own = row < N - lower
    operator = jnp.where(own, first_ref[pl.ds(lower, packed), :], second_ref[...])
    couple = operator // 2
    odd = operator % 2 == 1
    own = own[middle_row:]
    valid = row[middle_row:] <= N

    def at(lat, t, column):
        return pl.ds(lat * block + t * ROWS + column, count, stride=stride)

    def swap(x):
        return pltpu.roll(x, half, 1)

    def read_field(column):
        tiles = []
        for lat in range(0, lats, 2):
            low = field_all[at(lat, 2, column), :]
            high = field_all[at(lat + 1, 2, column), :]
            middle = [jnp.where(left, low, swap(high)), jnp.where(left, swap(low), high)]
            tiles.append([field_all[at(lat, t, column), :] for t in range(2)])
            tiles.append(middle)
            tiles.append([field_all[at(lat + 1, t, column), :] for t in range(2)])
        levels = [jnp.concatenate([tile[t] for tile in tiles], axis=1) for t in range(2)]
        return jnp.concatenate(levels, axis=0).astype(jnp.bfloat16)

    def write_field(column, value):
        for lat in range(0, lats, 2):
            first = lat // 2 * 3 * LANES
            tile = [value[:, first + i * LANES : first + (i + 1) * LANES] for i in range(3)]
            parts = [[x[:count], x[count:]] for x in tile]
            for t in range(2):
                out_all[at(lat, t, column), :] = parts[0][t]
                out_all[at(lat + 1, t, column), :] = parts[2][t]
            out_all[at(lat, 2, column), :] = jnp.where(left, parts[1][0], swap(parts[1][1]))
            out_all[at(lat + 1, 2, column), :] = jnp.where(left, swap(parts[1][0]), parts[1][1])

    for r in range(2):
        columns = [4 * pair + 2 * e + r for e in range(2)]
        tables = [table_ref.at[r, :N], table_ref.at[2 + r, middle_row:]]
        state = [dot(tables[e][...], read_field(columns[e]), ((1,), (1,))) for e in range(2)]
        upper = jnp.concatenate(
            [state[0][middle_row:], jnp.zeros((packed - N, LANES), jnp.float32)], axis=0
        )
        upper = jnp.where(own, upper, jnp.where(valid, state[1], 0.0))
        spectral = jnp.concatenate([state[0][:middle_row], upper], axis=0)
        spectral = spectral.astype(jnp.bfloat16).astype(jnp.float32)
        spread = [jnp.where(couple == g, spectral, 0.0).astype(jnp.bfloat16) for g in range(couples)]
        solved = dot(jnp.concatenate(spread, axis=1), vertical_ref[...], ((1,), (0,)))
        solved = jnp.where(odd, solved[:, LANES:], solved[:, :LANES])
        upper = solved[middle_row:]
        mine = [
            jnp.concatenate(
                [solved[:middle_row], jnp.where(own, upper, 0.0)[: N - middle_row]], axis=0
            ),
            jnp.where(own, 0.0, upper),
        ]
        for e in range(2):
            value = dot(mine[e].astype(jnp.bfloat16), tables[e][...], ((0,), (0,)))
            write_field(columns[e], value)

    @pl.when(pair == pl.num_programs(0) - 1)
    def _():
        out_ref[...] = out_all[: lats * block, :].astype(jnp.bfloat16).reshape(out_ref.shape)


def spectral_chunk(pieces, table, vertical, first, second, lower, chunk, shape, *ready):
    lats, levs, wire_rows, _ = shape
    columns, packed, all_lats = table.shape
    pairs = ROWS // 4
    rows = lats * levs * wire_rows
    plane = pieces[0].shape[0]
    block = (plane, rows // plane // len(pieces), LANES)
    return pl.pallas_call(
        functools.partial(spectral_kernel, len(pieces)),
        out_shape=jax.ShapeDtypeStruct(shape, jnp.bfloat16),
        grid_spec=pltpu.PrefetchScalarGridSpec(
            num_scalar_prefetch=1,
            grid=(pairs,),
            in_specs=[pl.BlockSpec(block, lambda p, _: (0, 0, 0))] * len(pieces)
            + [
                pl.BlockSpec((4, packed, all_lats), lambda p, _: (chunk * pairs + p, 0, 0)),
                pl.BlockSpec(vertical.shape, lambda p, _: (0, 0)),
                pl.BlockSpec(first.shape, lambda p, _: (0, 0)),
                pl.BlockSpec(second.shape, lambda p, _: (0, 0)),
            ]
            + [ANYWHERE] * len(ready),
            out_specs=pl.BlockSpec(shape, lambda p, _: (0, 0, 0, 0)),
            scratch_shapes=[
                pltpu.VMEM((rows + 4 * ROWS, LANES), jnp.float32),
                pltpu.VMEM((rows + 4 * ROWS, LANES), jnp.float32),
            ],
        ),
        compiler_params=pltpu.CompilerParams(vmem_limit_bytes=VMEM),
        cost_estimate=LONG,
        name="spectral_chunk",
    )(lower, *pieces, table, vertical, first, second, *ready)


def synthesis_kernel(pieces, parity_ref, *refs):
    field_refs, (table_ref, wind_ref) = refs[:pieces], refs[pieces : pieces + 2]
    out_ref, lines_ref = refs[-2:]
    half = LANES // 2
    whole = pl.ds(pl.multiple_of(half * parity_ref[0], half), LANES)
    rest = pl.ds(pl.multiple_of(LANES * (1 - parity_ref[0]), half), half)
    fields = jnp.concatenate([ref[...].astype(jnp.float32) for ref in field_refs], axis=0)
    for t in range(6):
        tile = fields[:, t * ROWS : (t + 1) * ROWS, :].reshape(-1, LANES)
        lines_ref[t * LANES : (t + 1) * LANES, :] = tile.astype(jnp.bfloat16).T

    sums = dot(lines_ref[...], table_ref[...], ((1,), (0,)))

    def put(t, j, rows, value):
        gain = wind_ref[t, 0, j, rows, :].astype(jnp.float32)
        out_ref[t, 0, j, rows, :] = (value * gain).astype(jnp.bfloat16)

    for j in range(2):
        first = j * 3 * LANES
        for t in range(2):
            put(t, j, whole, sums[first + t * LANES : first + (t + 1) * LANES])
            start = first + 2 * LANES + t * half
            put(t, j, rest, sums[start : start + half])


def synthesis_part(fields, table, wind, parity, start, count, before):
    _, _, _, lat_rows, points = wind.shape
    columns = table.shape[0]
    rows = 6 * ROWS

    def field_spec(array, first):
        return pl.BlockSpec((array.shape[0], rows, LANES), lambda s, _: (0, first + s, 0))

    grid_spec = pl.BlockSpec(
        (2, 1, 2, lat_rows, points), lambda s, _: (0, start + s, 0, 0, 0)
    )
    in_specs = [field_spec(*f) for f in fields]
    in_specs += [
        pl.BlockSpec((columns, points), lambda s, _: (0, 0)),
        grid_spec,
    ]
    operands = [f for f, _ in fields] + [table, wind]
    aliases = {}
    if before is not None:
        in_specs.append(ANYWHERE)
        aliases = {1 + len(operands): 0}
        operands.append(before)
    return pl.pallas_call(
        functools.partial(synthesis_kernel, len(fields)),
        out_shape=jax.ShapeDtypeStruct(wind.shape, jnp.bfloat16),
        grid_spec=pltpu.PrefetchScalarGridSpec(
            num_scalar_prefetch=1,
            grid=(count,),
            in_specs=in_specs,
            out_specs=grid_spec,
            scratch_shapes=[pltpu.VMEM((6 * LANES, columns), jnp.bfloat16)],
        ),
        input_output_aliases=aliases,
        compiler_params=pltpu.CompilerParams(vmem_limit_bytes=VMEM),
        cost_estimate=LONG,
        name="synthesis_part",
    )(parity, *operands)


def after_kernel(*refs):
    del refs


def after(x, *ready):
    return pl.pallas_call(
        after_kernel,
        out_shape=jax.ShapeDtypeStruct(x.shape, x.dtype),
        in_specs=[ANYWHERE] * (1 + len(ready)),
        out_specs=ANYWHERE,
        input_output_aliases={0: 0},
        cost_estimate=LONG,
        name="after",
    )(x, *ready)


def join_kernel(count, *refs):
    out_ref = refs[-1]
    rows = refs[0].shape[1]
    for k in range(count):
        out_ref[:, k * rows : (k + 1) * rows, :] = refs[k][...]


def join_slots(pieces, *ready):
    plane, rows, _ = pieces[-1].shape
    all_rows = len(pieces) * rows
    return pl.pallas_call(
        functools.partial(join_kernel, len(pieces)),
        out_shape=jax.ShapeDtypeStruct((plane, all_rows, LANES), jnp.bfloat16),
        grid=(2,),
        in_specs=[pl.BlockSpec((plane // 2, rows, LANES), lambda s: (s, 0, 0))] * len(pieces)
        + [ANYWHERE] * len(ready),
        out_specs=pl.BlockSpec((plane // 2, all_rows, LANES), lambda s: (s, 0, 0)),
        cost_estimate=LONG,
        name="join_slots",
    )(*pieces, *ready)


def part_kernel(layers, cuts, *refs):
    in_ref, out_refs = refs[0], refs[len(refs) - len(cuts) * (layers - 1) :]
    rows = in_ref.shape[1] // layers
    for i, out_ref in enumerate(out_refs):
        p, k = divmod(i, layers - 1)
        start = (k + 1) * rows + cuts[p][0]
        out_ref[...] = in_ref[:, start : start + cuts[p][1], :]


def part_slots(joined, layers, cuts, *ready):
    plane, rows, _ = joined.shape
    cuts = cuts or [(0, rows // layers)]
    sizes = [size for _, size in cuts for _ in range(layers - 1)]
    slots = pl.pallas_call(
        functools.partial(part_kernel, layers, cuts),
        out_shape=[jax.ShapeDtypeStruct((plane, n, LANES), jnp.bfloat16) for n in sizes],
        grid=(2,),
        in_specs=[pl.BlockSpec((plane // 2, rows, LANES), lambda s: (s, 0, 0))]
        + [ANYWHERE] * len(ready),
        out_specs=[pl.BlockSpec((plane // 2, n, LANES), lambda s: (s, 0, 0)) for n in sizes],
        cost_estimate=LONG,
        name="part_slots",
    )(joined, *ready)
    return [slots[p * (layers - 1) : (p + 1) * (layers - 1)] for p in range(len(cuts))]


def turn_along_z(slots, sign):
    lev_devices = lax.axis_size("lev")
    moved = []
    for k, slot in enumerate(slots, 1):
        pairs = [(b, (b + sign * CORES * k) % lev_devices) for b in range(lev_devices)]
        moved.append(lax.ppermute(slot, "lev", pairs))
    return moved


def exchange_in_plane(x, groups):
    return lax.all_to_all(
        x, ("lat", "lev"), split_axis=0, concat_axis=0, tiled=True, axis_index_groups=groups
    )


def turned(x, axis, start):
    size = x.shape[axis]
    return lax.dynamic_slice_in_dim(jnp.concatenate([x, x], axis=axis), start, size, axis)


def pipelined_body(adjoint_grid, wind, legendre, vertical, pair_table, degree_matrix):
    level_rows, lat_rows, points = adjoint_grid.shape
    lats = lax.axis_size("lat")
    levs = lax.axis_size("lev")
    layers = levs // CORES
    plane = lats * CORES
    slots, all_lats, packed = legendre.shape
    matrices, levels, _ = vertical.shape
    chunks = slots // ROWS
    pairs = ROWS // 4
    steps = level_rows // 4
    wire_rows = steps * 6 * ROWS

    lat, lev = lax.axis_index("lat"), lax.axis_index("lev")
    layer = lev // CORES
    parity = (lat % 2).astype(jnp.int32).reshape(1)
    groups = [
        [a * levs + z * CORES + c for a in range(lats) for c in range(CORES)] for z in range(layers)
    ]

    table_pairs = turned(pair_table.reshape(lats, layers, CORES, chunks, pairs), 1, layer)
    table_pairs = table_pairs.transpose(3, 1, 0, 2, 4)
    waves = jnp.stack([table_pairs, N - 1 - table_pairs], axis=-1)
    waves = jnp.broadcast_to(waves[..., None], waves.shape + (2,))
    waves = waves.reshape(chunks, layers, plane, ROWS)

    grid = adjoint_grid.reshape(2, steps, 2, lat_rows, points)
    wind = wind.reshape(2, steps, 2, lat_rows, points)
    table = legendre.transpose(0, 2, 1)

    slot_level = jnp.arange(levels, dtype=jnp.int32).reshape(layers, CORES, 2, level_rows // 2)
    slot_level = turned(jnp.flip(slot_level, 0), 0, layers - 1 - layer)
    slot_level = slot_level.transpose(2, 1, 0, 3).reshape(levels)
    order = (slot_level[:, None] == jnp.arange(levels)[None, :]).astype(jnp.bfloat16)
    operators = jnp.einsum("av,gvo->gao", order, vertical, preferred_element_type=jnp.float32)
    operators = jnp.einsum(
        "gao,bo->gab", operators.astype(jnp.bfloat16), order, preferred_element_type=jnp.float32
    )
    operators = operators.astype(jnp.bfloat16).reshape(matrices // 2, 2, levels, levels)
    operators = operators.transpose(0, 2, 1, 3).reshape(matrices // 2 * levels, 2 * levels)

    by_degree = jnp.concatenate([degree_matrix, jnp.broadcast_to(degree_matrix[-1:], (packed,))])
    second = jnp.concatenate([degree_matrix[:1], by_degree[: packed - 1]])
    first = jnp.broadcast_to(by_degree[:, None], (by_degree.shape[0], LANES))
    second = jnp.broadcast_to(second[:, None], (packed, LANES))
    first_pair = (lat * levs + lev) * (slots // 4)
    lower = lax.dynamic_slice(pair_table, (first_pair,), (slots // 4,)).reshape(chunks, pairs)

    joined_shape = (plane, layers * wire_rows, LANES)

    def across(x):
        return exchange_in_plane(x, groups)

    def along(first_slot, slots):
        return [first_slot] + turn_along_z(slots, 1)

    def home(first_slot, slots):
        return [first_slot] + turn_along_z(slots, -1)

    def solve(q, pieces, *ready):
        shape = (lats, levs, wire_rows, LANES)
        x = spectral_chunk(pieces, table, operators, first, second, lower[q], q, shape, *ready)
        return x.reshape(joined_shape)

    turned_waves = waves.transpose(0, 2, 1, 3)
    sent = fourier_some(grid, waves[0].reshape(-1, 1), parity, [plane] * layers)
    z0 = along(sent[0], sent[1:layers])
    rows = turned_waves[2].reshape(-1, 1)
    x2 = fourier_some(grid, rows, parity, [plane * layers], sent[0])[0].reshape(joined_shape)
    rows = turned_waves[1].reshape(-1, 1)
    x1 = fourier_some(grid, rows, parity, [plane * layers], x2)[0].reshape(joined_shape)
    p2 = across(x2)
    u1 = [after(x, *z0[1:]) for x in part_slots(x1, layers, None)[0]]
    z1 = along(x1, u1)
    j0 = after(join_slots(z0, *u1), p2)
    p0 = across(j0)
    u2 = part_slots(p2, layers, None, j0)[0]
    z2 = along(p2, u2)
    rows = turned_waves[3].reshape(-1, 1)
    x3 = fourier_some(grid, rows, parity, [plane * layers], u2[0])[0].reshape(joined_shape)
    rows = jnp.stack([waves[0], waves[2], waves[3], waves[1]]).reshape(-1, 1)
    synthesis = synthesis_rows(rows, points, ROWS * layers * plane, x3)
    x3 = after(x3, p0, synthesis)
    p3 = across(x3)
    s0 = solve(0, [p0], x3)
    j1 = join_slots(z1, s0)
    s0 = after(s0, p3)
    r0 = across(s0)
    u3 = part_slots(p3, layers, None, s0, j1)[0]
    z3 = along(p3, u3)
    j1 = after(j1, r0, u3[0])
    p1 = across(j1)
    b0 = part_slots(r0, layers, None, j1)[0]
    back0 = home(r0, b0)
    s2 = after(solve(2, z2, b0[0]), p1)
    r2 = across(s2)
    s3 = after(solve(3, z3, s2), r2)
    r3 = across(s3)
    b2 = part_slots(r2, layers, None, s3)[0]
    back2 = home(r2, b2)
    s1 = after(solve(1, [p1], b2[0]), r3)
    r1 = across(s1)
    b3 = part_slots(r3, layers, None, s1)[0]
    back3 = home(r3, b3)
    parts = [(0, steps // 2), (steps // 2, steps // 2)] if steps % 2 == 0 else [(0, steps)]
    cuts = [(6 * ROWS * first, 6 * ROWS * count) for first, count in parts]
    late = [home(r1, part) for part in part_slots(r1, layers, cuts, b3[0])]

    out = None
    for (first, count), part in zip(parts, late):
        here = [(f, first) for f in [*back0, *back2, *back3, part[0]]]
        here += [(f, 0) for f in part[1:]]
        out = synthesis_part(here, synthesis, wind, parity, first, count, out)
    return out.reshape(level_rows, lat_rows, points)


def body(adjoint_grid, wind, legendre, vertical, pair_table, degree_matrix):
    level_rows, lat_rows, points = adjoint_grid.shape
    lats, levs = lax.axis_size("lat"), lax.axis_size("lev")
    layers = levs // CORES
    fits = (
        levs % CORES == 0
        and lats % 2 == 0
        and lat_rows == LANES + LANES // 2
        and level_rows % 16 == 0
        and vertical.shape[0] % 2 == 0
        and vertical.shape[1] == LANES
        and points % LANES == 0
        and points // LANES <= LANES
        and legendre.shape[0] % ROWS == 0
        and legendre.shape[0] // ROWS == 4
        and legendre.shape[2] % 8 == 0
        and legendre.shape[2] > N
        and pair_table.shape[0] * 4 == legendre.shape[0] * lats * levs
    )
    plan = pipelined_body if fits else general_body
    return plan(adjoint_grid, wind, legendre, vertical, pair_table, degree_matrix)


def solution(mesh):
    placed = (
        P("lev", "lat", None),
        P("lev", "lat", None),
        P(("lat", "lev"), None, None),
        P(),
        P(),
        P(),
    )
    return jax.shard_map(
        body, mesh=mesh, in_specs=placed, out_specs=P("lev", "lat", None), check_vma=False
    )
```

```python
import functools
import math

import jax
import jax.numpy as jnp
from jax import lax
from jax.experimental import pallas as pl
from jax.experimental.pallas import tpu as pltpu
from jax.sharding import PartitionSpec as P

N = 512
CORES = 2
ROWS = 8
LANES = 128
VMEM = 48 * 2**20
LONG = pl.CostEstimate(flops=10**13, bytes_accessed=10**8, transcendentals=0)
SIN = (-1.0 / 39916800, 1.0 / 362880, -1.0 / 5040, 1.0 / 120, -1.0 / 6, 1.0)
ANYWHERE = pl.BlockSpec(memory_space=pl.ANY)


def fourier_basis(wavenumbers, points):
    longitude = jnp.arange(points, dtype=jnp.int32)
    phases = wavenumbers[:, :, None] * longitude[None, None, :] % points
    angles = phases.astype(jnp.float32) * (2.0 * jnp.pi / points)
    basis = jnp.stack([jnp.cos(angles), -jnp.sin(angles)], axis=2)
    return basis.reshape(-1, points)


def member_layout(lower_wave, row_total):
    packed_buffer = jnp.arange(row_total, dtype=jnp.int32)
    first_member = packed_buffer[None, :] < (N - lower_wave)[:, None]
    second_member = jnp.logical_not(first_member) & (packed_buffer[None, :] <= N)
    degree = jnp.where(
        first_member, lower_wave[:, None] + packed_buffer[None, :], packed_buffer[None, :] - 1
    )
    degree = jnp.clip(degree, 0, N - 1)
    return (first_member, second_member, degree)


def solve_columns(spectral_state, matrix_index, vertical):

    def add_matrix(operator_index, running):
        product = jnp.einsum(
            "xjm,mg->xjg",
            spectral_state,
            vertical[operator_index],
            preferred_element_type=jnp.float32,
        )
        return running + jnp.where((matrix_index == operator_index)[:, :, None], product, 0.0)

    zero_sums = jnp.zeros(spectral_state.shape, jnp.float32)
    return lax.fori_loop(0, vertical.shape[0], add_matrix, zero_sums).astype(jnp.bfloat16)


def general_body(adjoint_grid, wind, legendre, vertical, pair_table, degree_matrix):
    vertical_level_rows, lat_rows, points = adjoint_grid.shape
    lat_devices = lax.axis_size("lat")
    lev_devices = lax.axis_size("lev")
    slots = legendre.shape[0]
    all_lats = legendre.shape[1]
    packed_rows = legendre.shape[2]
    levels = vertical.shape[1]
    wavenumbers = jnp.stack([pair_table, N - 1 - pair_table], axis=1)
    basis = fourier_basis(wavenumbers, points)
    analysis_table = (basis * (1.0 / math.sqrt(points))).astype(jnp.bfloat16)
    synthesis_table = (basis * (1.0 / math.sqrt(N))).astype(jnp.bfloat16)
    fourier = jnp.einsum(
        "cx,vlx->cvl", analysis_table, adjoint_grid, preferred_element_type=jnp.float32
    )
    fourier = fourier.astype(jnp.bfloat16).reshape(
        lat_devices, lev_devices, slots, vertical_level_rows, lat_rows
    )
    moved = lax.all_to_all(
        lax.all_to_all(fourier, "lev", split_axis=1, concat_axis=3, tiled=True),
        "lat",
        split_axis=0,
        concat_axis=4,
        tiled=True,
    )
    field_stack = moved.reshape(slots, levels, all_lats)
    first_slot = (lax.axis_index("lat") * lev_devices + lax.axis_index("lev")) * slots
    column = first_slot + jnp.arange(slots, dtype=jnp.int32)
    lower_cols = jnp.take(pair_table, column // 4)
    member = column // 2 % 2
    first_member, second_member, degree = member_layout(lower_cols, packed_rows)
    own_rows = jnp.where((member == 0)[:, None], first_member, second_member).astype(jnp.float32)
    spectral_state = jnp.einsum(
        "peq,pae->pqa", legendre, field_stack, preferred_element_type=jnp.float32
    )
    spectral_state = (spectral_state * own_rows[:, :, None]).astype(jnp.bfloat16)
    matrix_index = jnp.take(degree_matrix, degree)
    solved_columns = solve_columns(spectral_state, matrix_index, vertical)
    gridpoint_coefficients = jnp.einsum(
        "ncb,nba->nac", legendre, solved_columns, preferred_element_type=jnp.float32
    )
    gridpoint_coefficients = gridpoint_coefficients.astype(jnp.bfloat16).reshape(
        1, 1, slots, levels, all_lats
    )
    returned = lax.all_to_all(
        lax.all_to_all(gridpoint_coefficients, "lat", split_axis=4, concat_axis=0, tiled=True),
        "lev",
        split_axis=3,
        concat_axis=1,
        tiled=True,
    )
    columns = returned.reshape(lat_devices * lev_devices * slots, vertical_level_rows, lat_rows)
    regridded = jnp.einsum(
        "cvl,cx->vlx", columns, synthesis_table, preferred_element_type=jnp.float32
    )
    return (regridded * wind.astype(jnp.float32)).astype(jnp.bfloat16)


def dot(a, b, dims):
    return lax.dot_general(a, b, (dims, ((), ())), preferred_element_type=jnp.float32)


def cos_turn(steps, points):
    rest = steps - points * jnp.floor(steps * (1.0 / points) + 0.5)
    angle = (points // 4 - jnp.abs(rest)) * (2.0 * math.pi / points)
    square = angle * angle
    total = jnp.full_like(square, SIN[0])
    for c in SIN[1:]:
        total = total * square + c
    return total * angle


def make_table(wave, points, scale):
    rows = wave.shape[0]
    lane = lax.broadcasted_iota(jnp.int32, (rows, LANES), 1).astype(jnp.float32)
    part = lax.broadcasted_iota(jnp.int32, (rows, LANES), 0) % 2
    shift = (part * (points // 4)).astype(jnp.float32)
    waves = jnp.broadcast_to(wave, (rows, LANES)).astype(jnp.float32)
    twice = 2.0 * cos_turn(waves * LANES, points)
    tiles = [cos_turn(waves * (lane + i * LANES) + shift, points) * scale for i in range(2)]
    while len(tiles) < points // LANES:
        tiles.append(twice * tiles[-1] - tiles[-2])
    return jnp.concatenate(tiles, axis=1).astype(jnp.bfloat16)


def fourier_kernel(waits, parity_ref, wave_ref, grid_ref, *refs):
    out_refs, table_ref = refs[waits:-1], refs[-1]
    points = grid_ref.shape[-1]
    rows = sum(ref.shape[0] for ref in out_refs) * ROWS

    @pl.when(pl.program_id(0) == 0)
    def _():
        block = ROWS * 32

        def fill(i, _):
            at = pl.ds(pl.multiple_of(i * block, block), block)
            table_ref[at, :] = make_table(wave_ref[at, :], points, 1.0 / math.sqrt(points))
            return 0

        lax.fori_loop(0, rows // block, fill, 0)

    half = LANES // 2
    whole = pl.ds(pl.multiple_of(half * parity_ref[0], half), LANES)
    rest = pl.ds(pl.multiple_of(LANES * (1 - parity_ref[0]), half), half)
    lines = []
    for j in range(2):
        lines += [grid_ref[t, 0, j, whole, :] for t in range(2)]
        lines += [grid_ref[t, 0, j, rest, :] for t in range(2)]
    lines = jnp.concatenate(lines, axis=0)
    sums = dot(table_ref[...], lines, ((1,), (1,)))
    sums = sums.reshape(-1, ROWS, sums.shape[1])
    start = 0
    for ref in out_refs:
        part = sums[start : start + ref.shape[0]]
        tiles = [part[:, :, t * LANES : (t + 1) * LANES] for t in range(6)]
        ref[...] = jnp.concatenate(tiles, axis=1).astype(jnp.bfloat16)
        start += ref.shape[0]


def fourier_some(grid, wave, parity, slots, *ready):
    _, steps, _, lat_rows, points = grid.shape
    columns = wave.shape[0]
    rows = 6 * ROWS
    return pl.pallas_call(
        functools.partial(fourier_kernel, len(ready)),
        out_shape=[jax.ShapeDtypeStruct((n, steps * rows, LANES), jnp.bfloat16) for n in slots],
        grid_spec=pltpu.PrefetchScalarGridSpec(
            num_scalar_prefetch=1,
            grid=(steps,),
            in_specs=[
                pl.BlockSpec((columns, 1), lambda s, _: (0, 0)),
                pl.BlockSpec((2, 1, 2, lat_rows, points), lambda s, _: (0, s, 0, 0, 0)),
            ]
            + [ANYWHERE] * len(ready),
            out_specs=[pl.BlockSpec((n, rows, LANES), lambda s, _: (0, s, 0)) for n in slots],
            scratch_shapes=[pltpu.VMEM((columns, points), jnp.bfloat16)],
        ),
        compiler_params=pltpu.CompilerParams(vmem_limit_bytes=VMEM),
        cost_estimate=LONG,
        name="fourier_some",
    )(parity, wave, grid, *ready)


def table_kernel(wave_ref, *refs):
    out_ref = refs[-1]
    out_ref[...] = make_table(wave_ref[...], out_ref.shape[1], 1.0 / math.sqrt(N))


def synthesis_rows(wave, points, block, *ready):
    columns = wave.shape[0]
    return pl.pallas_call(
        table_kernel,
        out_shape=jax.ShapeDtypeStruct((columns, points), jnp.bfloat16),
        grid=(columns // block,),
        in_specs=[pl.BlockSpec((block, 1), lambda s: (s, 0))] + [ANYWHERE] * len(ready),
        out_specs=pl.BlockSpec((block, points), lambda s: (s, 0)),
        compiler_params=pltpu.CompilerParams(vmem_limit_bytes=VMEM),
        cost_estimate=LONG,
        name="synthesis_rows",
    )(wave, *ready)


def spectral_kernel(pieces, lower_ref, *refs):
    field_refs = refs[:pieces]
    table_ref, vertical_ref, first_ref, second_ref = refs[pieces : pieces + 4]
    out_ref, field_all, out_all = refs[-3:]
    pair = pl.program_id(0)
    lats, levs, wire_rows, _ = out_ref.shape
    stride = 3 * ROWS
    count = levs * wire_rows // stride
    block = levs * wire_rows
    half = LANES // 2
    packed = table_ref.shape[1]
    couples = vertical_ref.shape[0] // LANES
    middle_row = N // 2

    @pl.when(pair == 0)
    def _():
        plane, rows, _ = field_refs[0].shape
        for i in range(plane):
            for k, ref in enumerate(field_refs):
                start = (i * pieces + k) * rows
                field_all[start : start + rows, :] = ref[i].astype(jnp.float32)

    left = lax.broadcasted_iota(jnp.int32, (count, LANES), 1) < half
    lower = lower_ref[pair]
    row = lax.broadcasted_iota(jnp.int32, (packed, LANES), 0)
    own = row < N - lower
    operator = jnp.where(own, first_ref[pl.ds(lower, packed), :], second_ref[...])
    couple = operator // 2
    odd = operator % 2 == 1
    own = own[middle_row:]
    valid = row[middle_row:] <= N

    def at(lat, t, column):
        return pl.ds(lat * block + t * ROWS + column, count, stride=stride)

    def swap(x):
        return pltpu.roll(x, half, 1)

    def read_field(column):
        tiles = []
        for lat in range(0, lats, 2):
            low = field_all[at(lat, 2, column), :]
            high = field_all[at(lat + 1, 2, column), :]
            middle = [jnp.where(left, low, swap(high)), jnp.where(left, swap(low), high)]
            tiles.append([field_all[at(lat, t, column), :] for t in range(2)])
            tiles.append(middle)
            tiles.append([field_all[at(lat + 1, t, column), :] for t in range(2)])
        levels = [jnp.concatenate([tile[t] for tile in tiles], axis=1) for t in range(2)]
        return jnp.concatenate(levels, axis=0).astype(jnp.bfloat16)

    def write_field(column, value):
        for lat in range(0, lats, 2):
            first = lat // 2 * 3 * LANES
            tile = [value[:, first + i * LANES : first + (i + 1) * LANES] for i in range(3)]
            parts = [[x[:count], x[count:]] for x in tile]
            for t in range(2):
                out_all[at(lat, t, column), :] = parts[0][t]
                out_all[at(lat + 1, t, column), :] = parts[2][t]
            out_all[at(lat, 2, column), :] = jnp.where(left, parts[1][0], swap(parts[1][1]))
            out_all[at(lat + 1, 2, column), :] = jnp.where(left, swap(parts[1][0]), parts[1][1])

    for r in range(2):
        columns = [4 * pair + 2 * e + r for e in range(2)]
        tables = [table_ref.at[r, :N], table_ref.at[2 + r, middle_row:]]
        state = [dot(tables[e][...], read_field(columns[e]), ((1,), (1,))) for e in range(2)]
        upper = jnp.concatenate(
            [state[0][middle_row:], jnp.zeros((packed - N, LANES), jnp.float32)], axis=0
        )
        upper = jnp.where(own, upper, jnp.where(valid, state[1], 0.0))
        spectral = jnp.concatenate([state[0][:middle_row], upper], axis=0)
        spectral = spectral.astype(jnp.bfloat16).astype(jnp.float32)
        spread = [jnp.where(couple == g, spectral, 0.0).astype(jnp.bfloat16) for g in range(couples)]
        solved = dot(jnp.concatenate(spread, axis=1), vertical_ref[...], ((1,), (0,)))
        solved = jnp.where(odd, solved[:, LANES:], solved[:, :LANES])
        upper = solved[middle_row:]
        mine = [
            jnp.concatenate(
                [solved[:middle_row], jnp.where(own, upper, 0.0)[: N - middle_row]], axis=0
            ),
            jnp.where(own, 0.0, upper),
        ]
        for e in range(2):
            value = dot(mine[e].astype(jnp.bfloat16), tables[e][...], ((0,), (0,)))
            write_field(columns[e], value)

    @pl.when(pair == pl.num_programs(0) - 1)
    def _():
        out_ref[...] = out_all[: lats * block, :].astype(jnp.bfloat16).reshape(out_ref.shape)


def spectral_chunk(pieces, table, vertical, first, second, lower, chunk, shape, *ready):
    lats, levs, wire_rows, _ = shape
    columns, packed, all_lats = table.shape
    pairs = ROWS // 4
    rows = lats * levs * wire_rows
    plane = pieces[0].shape[0]
    block = (plane, rows // plane // len(pieces), LANES)
    return pl.pallas_call(
        functools.partial(spectral_kernel, len(pieces)),
        out_shape=jax.ShapeDtypeStruct(shape, jnp.bfloat16),
        grid_spec=pltpu.PrefetchScalarGridSpec(
            num_scalar_prefetch=1,
            grid=(pairs,),
            in_specs=[pl.BlockSpec(block, lambda p, _: (0, 0, 0))] * len(pieces)
            + [
                pl.BlockSpec((4, packed, all_lats), lambda p, _: (chunk * pairs + p, 0, 0)),
                pl.BlockSpec(vertical.shape, lambda p, _: (0, 0)),
                pl.BlockSpec(first.shape, lambda p, _: (0, 0)),
                pl.BlockSpec(second.shape, lambda p, _: (0, 0)),
            ]
            + [ANYWHERE] * len(ready),
            out_specs=pl.BlockSpec(shape, lambda p, _: (0, 0, 0, 0)),
            scratch_shapes=[
                pltpu.VMEM((rows + 4 * ROWS, LANES), jnp.float32),
                pltpu.VMEM((rows + 4 * ROWS, LANES), jnp.float32),
            ],
        ),
        compiler_params=pltpu.CompilerParams(vmem_limit_bytes=VMEM),
        cost_estimate=LONG,
        name="spectral_chunk",
    )(lower, *pieces, table, vertical, first, second, *ready)


def synthesis_kernel(pieces, parity_ref, *refs):
    field_refs, (table_ref, wind_ref) = refs[:pieces], refs[pieces : pieces + 2]
    out_ref, lines_ref = refs[-2:]
    half = LANES // 2
    whole = pl.ds(pl.multiple_of(half * parity_ref[0], half), LANES)
    rest = pl.ds(pl.multiple_of(LANES * (1 - parity_ref[0]), half), half)
    fields = jnp.concatenate([ref[...].astype(jnp.float32) for ref in field_refs], axis=0)
    for t in range(6):
        tile = fields[:, t * ROWS : (t + 1) * ROWS, :].reshape(-1, LANES)
        lines_ref[t * LANES : (t + 1) * LANES, :] = tile.astype(jnp.bfloat16).T

    sums = dot(lines_ref[...], table_ref[...], ((1,), (0,)))

    def put(t, j, rows, value):
        gain = wind_ref[t, 0, j, rows, :].astype(jnp.float32)
        out_ref[t, 0, j, rows, :] = (value * gain).astype(jnp.bfloat16)

    for j in range(2):
        first = j * 3 * LANES
        for t in range(2):
            put(t, j, whole, sums[first + t * LANES : first + (t + 1) * LANES])
            start = first + 2 * LANES + t * half
            put(t, j, rest, sums[start : start + half])


def synthesis_part(fields, table, wind, parity, start, count, before):
    _, _, _, lat_rows, points = wind.shape
    columns = table.shape[0]
    rows = 6 * ROWS

    def field_spec(array, first):
        return pl.BlockSpec((array.shape[0], rows, LANES), lambda s, _: (0, first + s, 0))

    grid_spec = pl.BlockSpec(
        (2, 1, 2, lat_rows, points), lambda s, _: (0, start + s, 0, 0, 0)
    )
    in_specs = [field_spec(*f) for f in fields]
    in_specs += [
        pl.BlockSpec((columns, points), lambda s, _: (0, 0)),
        grid_spec,
    ]
    operands = [f for f, _ in fields] + [table, wind]
    aliases = {}
    if before is not None:
        in_specs.append(ANYWHERE)
        aliases = {1 + len(operands): 0}
        operands.append(before)
    return pl.pallas_call(
        functools.partial(synthesis_kernel, len(fields)),
        out_shape=jax.ShapeDtypeStruct(wind.shape, jnp.bfloat16),
        grid_spec=pltpu.PrefetchScalarGridSpec(
            num_scalar_prefetch=1,
            grid=(count,),
            in_specs=in_specs,
            out_specs=grid_spec,
            scratch_shapes=[pltpu.VMEM((6 * LANES, columns), jnp.bfloat16)],
        ),
        input_output_aliases=aliases,
        compiler_params=pltpu.CompilerParams(vmem_limit_bytes=VMEM // 3 * 2),
        cost_estimate=LONG,
        name="synthesis_part",
    )(parity, *operands)


def after_kernel(*refs):
    del refs


def after(x, *ready):
    return pl.pallas_call(
        after_kernel,
        out_shape=jax.ShapeDtypeStruct(x.shape, x.dtype),
        in_specs=[ANYWHERE] * (1 + len(ready)),
        out_specs=ANYWHERE,
        input_output_aliases={0: 0},
        cost_estimate=LONG,
        name="after",
    )(x, *ready)


def join_kernel(count, *refs):
    out_ref = refs[-1]
    rows = refs[0].shape[1]
    for k in range(count):
        out_ref[:, k * rows : (k + 1) * rows, :] = refs[k][...]


def join_slots(pieces, *ready):
    plane, rows, _ = pieces[-1].shape
    all_rows = len(pieces) * rows
    return pl.pallas_call(
        functools.partial(join_kernel, len(pieces)),
        out_shape=jax.ShapeDtypeStruct((plane, all_rows, LANES), jnp.bfloat16),
        grid=(2,),
        in_specs=[pl.BlockSpec((plane // 2, rows, LANES), lambda s: (s, 0, 0))] * len(pieces)
        + [ANYWHERE] * len(ready),
        out_specs=pl.BlockSpec((plane // 2, all_rows, LANES), lambda s: (s, 0, 0)),
        cost_estimate=LONG,
        name="join_slots",
    )(*pieces, *ready)


def part_kernel(layers, cuts, *refs):
    in_ref, out_refs = refs[0], refs[len(refs) - len(cuts) * (layers - 1) :]
    rows = in_ref.shape[1] // layers
    for i, out_ref in enumerate(out_refs):
        p, k = divmod(i, layers - 1)
        start = (k + 1) * rows + cuts[p][0]
        out_ref[...] = in_ref[:, start : start + cuts[p][1], :]


def part_slots(joined, layers, cuts, *ready):
    plane, rows, _ = joined.shape
    cuts = cuts or [(0, rows // layers)]
    sizes = [size for _, size in cuts for _ in range(layers - 1)]
    slots = pl.pallas_call(
        functools.partial(part_kernel, layers, cuts),
        out_shape=[jax.ShapeDtypeStruct((plane, n, LANES), jnp.bfloat16) for n in sizes],
        grid=(2,),
        in_specs=[pl.BlockSpec((plane // 2, rows, LANES), lambda s: (s, 0, 0))]
        + [ANYWHERE] * len(ready),
        out_specs=[pl.BlockSpec((plane // 2, n, LANES), lambda s: (s, 0, 0)) for n in sizes],
        cost_estimate=LONG,
        name="part_slots",
    )(joined, *ready)
    return [slots[p * (layers - 1) : (p + 1) * (layers - 1)] for p in range(len(cuts))]


def turn_along_z(slots, sign):
    lev_devices = lax.axis_size("lev")
    moved = []
    for k, slot in enumerate(slots, 1):
        pairs = [(b, (b + sign * CORES * k) % lev_devices) for b in range(lev_devices)]
        moved.append(lax.ppermute(slot, "lev", pairs))
    return moved


def exchange_in_plane(x, groups):
    return lax.all_to_all(
        x, ("lat", "lev"), split_axis=0, concat_axis=0, tiled=True, axis_index_groups=groups
    )


def turned(x, axis, start):
    size = x.shape[axis]
    return lax.dynamic_slice_in_dim(jnp.concatenate([x, x], axis=axis), start, size, axis)


def pipelined_body(adjoint_grid, wind, legendre, vertical, pair_table, degree_matrix):
    level_rows, lat_rows, points = adjoint_grid.shape
    lats = lax.axis_size("lat")
    levs = lax.axis_size("lev")
    layers = levs // CORES
    plane = lats * CORES
    slots, all_lats, packed = legendre.shape
    matrices, levels, _ = vertical.shape
    chunks = slots // ROWS
    pairs = ROWS // 4
    steps = level_rows // 4
    wire_rows = steps * 6 * ROWS

    lat, lev = lax.axis_index("lat"), lax.axis_index("lev")
    layer = lev // CORES
    parity = (lat % 2).astype(jnp.int32).reshape(1)
    groups = [
        [a * levs + z * CORES + c for a in range(lats) for c in range(CORES)] for z in range(layers)
    ]

    table_pairs = turned(pair_table.reshape(lats, layers, CORES, chunks, pairs), 1, layer)
    table_pairs = table_pairs.transpose(3, 1, 0, 2, 4)
    waves = jnp.stack([table_pairs, N - 1 - table_pairs], axis=-1)
    waves = jnp.broadcast_to(waves[..., None], waves.shape + (2,))
    waves = waves.reshape(chunks, layers, plane, ROWS)

    grid = adjoint_grid.reshape(2, steps, 2, lat_rows, points)
    wind = wind.reshape(2, steps, 2, lat_rows, points)
    table = legendre.transpose(0, 2, 1)

    slot_level = jnp.arange(levels, dtype=jnp.int32).reshape(layers, CORES, 2, level_rows // 2)
    slot_level = turned(jnp.flip(slot_level, 0), 0, layers - 1 - layer)
    slot_level = slot_level.transpose(2, 1, 0, 3).reshape(levels)
    order = (slot_level[:, None] == jnp.arange(levels)[None, :]).astype(jnp.bfloat16)
    operators = jnp.einsum("av,gvo->gao", order, vertical, preferred_element_type=jnp.float32)
    operators = jnp.einsum(
        "gao,bo->gab", operators.astype(jnp.bfloat16), order, preferred_element_type=jnp.float32
    )
    operators = operators.astype(jnp.bfloat16).reshape(matrices // 2, 2, levels, levels)
    operators = operators.transpose(0, 2, 1, 3).reshape(matrices // 2 * levels, 2 * levels)

    by_degree = jnp.concatenate([degree_matrix, jnp.broadcast_to(degree_matrix[-1:], (packed,))])
    second = jnp.concatenate([degree_matrix[:1], by_degree[: packed - 1]])
    first = jnp.broadcast_to(by_degree[:, None], (by_degree.shape[0], LANES))
    second = jnp.broadcast_to(second[:, None], (packed, LANES))
    first_pair = (lat * levs + lev) * (slots // 4)
    lower = lax.dynamic_slice(pair_table, (first_pair,), (slots // 4,)).reshape(chunks, pairs)

    joined_shape = (plane, layers * wire_rows, LANES)

    def across(x):
        return exchange_in_plane(x, groups)

    def along(first_slot, slots):
        return [first_slot] + turn_along_z(slots, 1)

    def home(first_slot, slots):
        return [first_slot] + turn_along_z(slots, -1)

    def solve(q, pieces, *ready):
        shape = (lats, levs, wire_rows, LANES)
        x = spectral_chunk(pieces, table, operators, first, second, lower[q], q, shape, *ready)
        return x.reshape(joined_shape)

    turned_waves = waves.transpose(0, 2, 1, 3)
    sent = fourier_some(grid, waves[0].reshape(-1, 1), parity, [plane] * layers)
    z0 = along(sent[0], sent[1:layers])
    rows = turned_waves[2].reshape(-1, 1)
    x2 = fourier_some(grid, rows, parity, [plane * layers], sent[0])[0].reshape(joined_shape)
    rows = turned_waves[1].reshape(-1, 1)
    x1 = fourier_some(grid, rows, parity, [plane * layers], x2)[0].reshape(joined_shape)
    p2 = across(x2)
    u1 = [after(x, *z0[1:]) for x in part_slots(x1, layers, None)[0]]
    z1 = along(x1, u1)
    j0 = after(join_slots(z0, *u1), p2)
    p0 = across(j0)
    u2 = part_slots(p2, layers, None, j0)[0]
    z2 = along(p2, u2)
    rows = turned_waves[3].reshape(-1, 1)
    x3 = fourier_some(grid, rows, parity, [plane * layers], u2[0])[0].reshape(joined_shape)
    rows = jnp.stack([waves[0], waves[2], waves[3], waves[1]]).reshape(-1, 1)
    synthesis = synthesis_rows(rows, points, ROWS * layers * plane, x3)
    x3 = after(x3, p0, synthesis)
    p3 = across(x3)
    s0 = solve(0, [p0], x3)
    j1 = join_slots(z1, s0)
    s0 = after(s0, p3)
    r0 = across(s0)
    u3 = part_slots(p3, layers, None, s0, j1)[0]
    z3 = along(p3, u3)
    j1 = after(j1, r0, u3[0])
    p1 = across(j1)
    b0 = part_slots(r0, layers, None, j1)[0]
    back0 = home(r0, b0)
    s2 = after(solve(2, z2, b0[0]), p1)
    r2 = across(s2)
    s3 = after(solve(3, z3, s2), r2)
    r3 = across(s3)
    b2 = part_slots(r2, layers, None, s3)[0]
    back2 = home(r2, b2)
    s1 = after(solve(1, [p1], b2[0]), r3)
    r1 = across(s1)
    b3 = part_slots(r3, layers, None, s1)[0]
    back3 = home(r3, b3)
    parts = [(0, steps // 2), (steps // 2, steps // 2)] if steps % 2 == 0 else [(0, steps)]
    cuts = [(6 * ROWS * first, 6 * ROWS * count) for first, count in parts]
    late = [home(r1, part) for part in part_slots(r1, layers, cuts, b3[0])]

    out = None
    for (first, count), part in zip(parts, late):
        here = [(f, first) for f in [*back0, *back2, *back3, part[0]]]
        here += [(f, 0) for f in part[1:]]
        out = synthesis_part(here, synthesis, wind, parity, first, count, out)
    return out.reshape(level_rows, lat_rows, points)


def body(adjoint_grid, wind, legendre, vertical, pair_table, degree_matrix):
    level_rows, lat_rows, points = adjoint_grid.shape
    lats, levs = lax.axis_size("lat"), lax.axis_size("lev")
    layers = levs // CORES
    fits = (
        levs % CORES == 0
        and lats % 2 == 0
        and lat_rows == LANES + LANES // 2
        and level_rows % 16 == 0
        and vertical.shape[0] % 2 == 0
        and vertical.shape[1] == LANES
        and points % LANES == 0
        and points // LANES <= LANES
        and legendre.shape[0] % ROWS == 0
        and legendre.shape[0] // ROWS == 4
        and legendre.shape[2] % 8 == 0
        and legendre.shape[2] > N
        and pair_table.shape[0] * 4 == legendre.shape[0] * lats * levs
    )
    plan = pipelined_body if fits else general_body
    return plan(adjoint_grid, wind, legendre, vertical, pair_table, degree_matrix)


def solution(mesh):
    placed = (
        P("lev", "lat", None),
        P("lev", "lat", None),
        P(("lat", "lev"), None, None),
        P(),
        P(),
        P(),
    )
    return jax.shard_map(
        body, mesh=mesh, in_specs=placed, out_specs=P("lev", "lat", None), check_vma=False
    )
```
